32 devices in a mesh: scen: 8 (over z, x), rep: 4 (over y, core).
Axes of the slice: x: 2, y: 2, z: 4, core: 2. Of those that a mesh axis runs over, the one named last changes fastest.
Arguments:
- scenarios: bfloat16 [8192, 16384], P('scen', 'rep'), may hold values from -24 to 24, as said below
- rep_index: int32 [1024], replicated, may hold values from 0 to 8191, as said below
Outputs:
- scen_potential: float32 [8192], P('scen')
- rep_potential: float32 [1024], P('rep')
- membership: bfloat16 [1024, 8192], P('rep', 'scen')
The draws below stay inside these ranges and needn't reach their ends.
Inputs may be any that keep to these rules, and one draw needn't show every extreme that they name: `rep_index`: the entries are distinct scenario numbers; each aligned block of 1024 consecutive scenarios holds exactly 128 of them. `scenarios`: finite surge values.
All inputs are finite; a program needn't handle non-finite values.
Results may differ from the reference program's by a relative error of at most 0.0035.
Values may be sent and summed in bfloat16 or wider, within the bound.
No kernel may reach another device: no remote copies, remote signals or barrier semaphores. Data moves between devices by JAX's collectives and lax.ppermute only.
A program may use at most 64 MiB of HBM per device.

```python
import math
import jax
import jax.numpy as jnp
from jax import lax

S_DEV = 1024
F = 16384
ITERS = 3
S = 8192
R = 1024


def draw_scenarios(key, part):
    key_base = jax.random.fold_in(key, 11)
    key_z, key_s = jax.random.split(key_base, 2)
    noise = jnp.clip(jax.random.normal(key_z, (S, F), jnp.float32), -6.0, 6.0)
    scales = jnp.exp(jax.random.uniform(key_s, (S, 1), jnp.float32, jnp.log(0.5), jnp.log(2.0)))
    values = scales * noise
    return values.astype(jnp.bfloat16)


def draw_rep_index(key, part):
    key_base = jax.random.fold_in(key, 23)
    key_pick, key_order = jax.random.split(key_base)
    blocks = S // S_DEV
    per_block = R // blocks
    scores = jax.random.randint(key_pick, (blocks, S_DEV), 0, 2 ** 18, jnp.int32) * S_DEV
    scores = scores + jnp.arange(S_DEV, dtype=jnp.int32)[None, :]
    scores = scores.at[0, 0].set(-1)
    scores = scores.at[blocks - 1, S_DEV - 1].set(-2)
    picks = jnp.argsort(scores, axis=1)[:, :per_block].astype(jnp.int32)
    picks = picks + (jnp.arange(blocks, dtype=jnp.int32) * S_DEV)[:, None]
    flat = picks.reshape(R)
    order = jax.random.permutation(key_order, R)
    return flat[order].astype(jnp.int32)


def setup_inputs(seed: int = 0) -> dict:
    splits = jax.random.split(jax.random.key(seed), 3)
    scenarios = draw_scenarios(jax.random.fold_in(splits[2], 71), 0)
    rep_index = draw_rep_index(jax.random.fold_in(splits[2], 71), 0)
    return dict(scenarios=scenarios, rep_index=rep_index)


eps_blur = 0.1


def log_sum(score, axis):
    peak = jnp.max(score, axis=axis, keepdims=True)
    total = jnp.sum(jnp.exp(score - peak), axis=axis)
    return jnp.squeeze(peak, axis) + jnp.log(total)


def reference(scenarios, rep_index):
    reps = jnp.take(scenarios, rep_index, axis=0)
    sq_scen = jnp.sum(jnp.square(scenarios.astype(jnp.float32)), axis=1)
    sq_rep = jnp.sum(jnp.square(reps.astype(jnp.float32)), axis=1)
    cross = lax.dot_general(reps, scenarios, (((1,), (1,)), ((), ())), preferred_element_type=jnp.float32)
    cost = (sq_rep[:, None] + sq_scen[None, :] - 2.0 * cross) / F
    count_s = scenarios.shape[0]
    count_r = reps.shape[0]
    rep_pot = jnp.zeros((count_r,), jnp.float32)
    scen_pot = jnp.zeros((count_s,), jnp.float32)
    for step in range(ITERS):
        scen_pot = -eps_blur * math.log(count_s) - eps_blur * log_sum((rep_pot[:, None] - cost) / eps_blur, 0)
        rep_pot = -eps_blur * math.log(count_r) - eps_blur * log_sum((scen_pot[None, :] - cost) / eps_blur, 1)
    member = (count_s * jnp.exp((scen_pot[None, :] + rep_pot[:, None] - cost) / eps_blur)).astype(jnp.bfloat16)
    return scen_pot, rep_pot, member
```

```python
import functools
import math

import jax
import jax.numpy as jnp
from jax import lax
from jax.experimental import pallas as pl
from jax.experimental.pallas import tpu as pltpu
from jax.sharding import PartitionSpec as P

ITERS = 3
eps_blur = 0.1

LANES = 128
SUB = 8
NT = (((1,), (1,)), ((), ()))
VMEM = pl.BlockSpec(memory_space=pltpu.VMEM)
SMEM = pl.BlockSpec(memory_space=pltpu.SMEM)


def square_sums(x):
    gram = lax.dot_general(x, x, NT, preferred_element_type=jnp.float32)
    n = x.shape[0]
    eye = lax.broadcasted_iota(jnp.int32, (n, n), 0) == lax.broadcasted_iota(jnp.int32, (n, n), 1)
    return jnp.sum(jnp.where(eye, gram, 0.0), axis=0, keepdims=True)


def pick_kernel(sel_ref, scen_ref, out_ref, *, step):
    for at in range(0, scen_ref.shape[1], step):
        out_ref[:, at : at + step] = jnp.dot(
            sel_ref[...], scen_ref[:, at : at + step], preferred_element_type=jnp.float32
        ).astype(out_ref.dtype)


def pick(sel, scenarios):
    rows, width = sel.shape[0], scenarios.shape[1]
    return pl.pallas_call(
        functools.partial(pick_kernel, step=min(512, width)),
        out_shape=jax.ShapeDtypeStruct((rows, width), scenarios.dtype),
        in_specs=[VMEM] * 2,
        out_specs=VMEM,
        cost_estimate=pl.CostEstimate(
            flops=2 * rows * scenarios.size, bytes_accessed=2 * scenarios.size, transcendentals=0
        ),
        name="pick",
    )(sel, scenarios)


def norm_kernel(scen_ref, out_ref):
    def body(i, carry):
        rows = pl.ds(pl.multiple_of(i * 16, 16), 16)
        x = scen_ref[rows, :].astype(jnp.float32)
        out_ref[rows, :] = jnp.broadcast_to(jnp.sum(x * x, axis=1, keepdims=True), (16, LANES))
        return carry

    lax.fori_loop(0, scen_ref.shape[0] // 16, body, 0, unroll=2)


def norms(scenarios):
    return pl.pallas_call(
        norm_kernel,
        out_shape=jax.ShapeDtypeStruct((scenarios.shape[0], LANES), jnp.float32),
        in_specs=[VMEM],
        out_specs=VMEM,
        cost_estimate=pl.CostEstimate(
            flops=2 * scenarios.size, bytes_accessed=2 * scenarios.size, transcendentals=0
        ),
        name="norms",
    )(scenarios)


def cost_kernel(core_ref, scen_ref, sq_ref, *refs, tile):
    *chunks, send_ref, keep_ref = refs
    reps = jnp.concatenate([c[...] for c in chunks], axis=0)
    sq_rep = square_sums(reps)
    half = send_ref.shape[0]
    core = core_ref[0]
    for out_ref, which in ((send_ref, 1 - core), (keep_ref, core)):
        for at in range(0, half, tile):
            rows = pl.ds(pl.multiple_of(which * half + at, tile), tile)
            cross = lax.dot_general(scen_ref[rows, :], reps, NT, preferred_element_type=jnp.float32)
            out_ref[at : at + tile, :] = sq_rep + sq_ref[rows, 0:1] - 2.0 * cross


def cost_share(core, scenarios, sq_scen, chunks):
    rows, width = scenarios.shape
    cols = sum(c.shape[0] for c in chunks)
    half = jax.ShapeDtypeStruct((rows // 2, cols), jnp.float32)
    return pl.pallas_call(
        functools.partial(cost_kernel, tile=min(256, rows // 2)),
        out_shape=(half, half),
        in_specs=[SMEM] + [VMEM] * (2 + len(chunks)),
        out_specs=(VMEM, VMEM),
        cost_estimate=pl.CostEstimate(
            flops=2 * rows * cols * width, bytes_accessed=2 * rows * width, transcendentals=0
        ),
        name="cost_share",
    )(core, scenarios, sq_scen, *chunks)


def tree(op, xs):
    while len(xs) > 1:
        xs = [op(*xs[i : i + 2]) if i + 1 < len(xs) else xs[i] for i in range(0, len(xs), 2)]
    return xs[0]


def put_sums(acc, out_ref, shift):
    at = lax.broadcasted_iota(jnp.int32, (len(acc), LANES), 0)
    total = jnp.zeros((len(acc), LANES), jnp.float32)
    for i, a in enumerate(acc):
        total = jnp.where(at == i, jnp.sum(a, axis=0, keepdims=True), total)
    if shift is not None:
        total = pltpu.roll(total, shift, 0)
    for k in range(out_ref.shape[0]):
        out_ref[k] = total


def get_factors(got_ref, scale, shift):
    total = tree(jnp.add, [got_ref[k] for k in range(got_ref.shape[0])])
    if shift is not None:
        total = pltpu.roll(total, shift, 0)
    return scale / total


def spread(w):
    return [jnp.broadcast_to(w[i : i + 1, :], (SUB, LANES)) for i in range(w.shape[0])]


def first_kernel(ids_ref, *refs, pieces, scale, rolled):
    stages = len(refs) // 2 - 1
    mine, other = refs[:stages], refs[stages : 2 * stages]
    e_ref, peak_ref, out_ref = refs[2 * stages :]
    half = mine[0].shape[0]
    core = ids_ref[0]

    def body(i, acc, h):
        src = pl.ds(pl.multiple_of(i * SUB, SUB), SUB)
        dst = pl.ds(pl.multiple_of(h * half + i * SUB, SUB), SUB)
        z = []
        for s, at in pieces:
            cols = slice(at, at + LANES)
            z.append(jnp.where(core == h, mine[s][src, cols], other[s][src, cols]) * scale)
        peak = jnp.max(tree(jnp.maximum, z), axis=1, keepdims=True)
        e = [jnp.exp(x - peak) for x in z]
        q = 1.0 / jnp.sum(tree(jnp.add, e), axis=1, keepdims=True)
        for k, x in enumerate(e):
            e_ref[dst, k * LANES : (k + 1) * LANES] = x
        peak_ref[dst, :] = jnp.broadcast_to(peak, (SUB, LANES))
        return tuple(a + x * q for a, x in zip(acc, e, strict=True))

    acc = tuple(jnp.zeros((SUB, LANES), jnp.float32) for _ in pieces)
    for h in range(2):
        acc = lax.fori_loop(0, half // SUB, functools.partial(body, h=h), acc, unroll=4)
    put_sums(acc, out_ref, ids_ref[1] if rolled else None)


def step_kernel(ids_ref, got_ref, e_ref, out_ref, *, scale, rolled):
    tiles = e_ref.shape[1] // LANES
    w = spread(get_factors(got_ref, scale, ids_ref[2] if rolled else None))

    def body(i, acc):
        rows = pl.ds(pl.multiple_of(i * SUB, SUB), SUB)
        e = [e_ref[rows, k * LANES : (k + 1) * LANES] for k in range(tiles)]
        q = 1.0 / jnp.sum(tree(jnp.add, [x * f for x, f in zip(e, w)]), axis=1, keepdims=True)
        return tuple(a + x * q for a, x in zip(acc, e, strict=True))

    acc = tuple(jnp.zeros((SUB, LANES), jnp.float32) for _ in range(tiles))
    acc = lax.fori_loop(0, e_ref.shape[0] // SUB, body, acc, unroll=4)
    put_sums(acc, out_ref, ids_ref[1] if rolled else None)


def last_kernel(ids_ref, got_ref, e_ref, peak_ref, out_ref, pot_ref, scaled_ref, col_ref, *, scale, rolled, log_count):
    rows_all = e_ref.shape[0]
    tiles = e_ref.shape[1] // LANES
    w = spread(get_factors(got_ref, scale, ids_ref[2] if rolled else None))

    def body(i, acc):
        rows = pl.ds(pl.multiple_of(i * SUB, SUB), SUB)
        e = [e_ref[rows, k * LANES : (k + 1) * LANES] for k in range(tiles)]
        total = jnp.sum(tree(jnp.add, [x * f for x, f in zip(e, w)]), axis=1, keepdims=True)
        col_ref[rows, :] = -eps_blur * (log_count + peak_ref[rows, :] + jnp.log(total))
        e = [x * (1.0 / total) for x in e]
        for k, x in enumerate(e):
            scaled_ref[rows, k * LANES : (k + 1) * LANES] = x
        return tuple(a + x for a, x in zip(acc, e, strict=True))

    acc = tuple(jnp.zeros((SUB, LANES), jnp.float32) for _ in range(tiles))
    acc = lax.fori_loop(0, rows_all // SUB, body, acc, unroll=4)
    put_sums(acc, out_ref, ids_ref[1] if rolled else None)
    for i in range(rows_all // LANES):
        block = col_ref[i * LANES : (i + 1) * LANES, :]
        pot_ref[i : i + 1, :] = jnp.transpose(block)[0:1, :]


def out_kernel(ids_ref, got_ref, scaled_ref, perm_ref, pot_ref, member_ref, *, scale, rolled):
    tiles = scaled_ref.shape[1] // LANES
    factors = get_factors(got_ref, scale, ids_ref[2] if rolled else None)
    w = jnp.concatenate([factors[i : i + 1, :] for i in range(tiles)], axis=1)
    v = eps_blur * jnp.log(w)
    high = v.astype(jnp.bfloat16).astype(jnp.float32)
    mid = (v - high).astype(jnp.bfloat16).astype(jnp.float32)
    low = v - high - mid
    at = lax.broadcasted_iota(jnp.int32, (16, w.shape[1]), 0)
    parts = jnp.where(at == 0, high, jnp.where(at == 1, mid, jnp.where(at == 2, low, 0.0)))
    moved = lax.dot_general(
        parts.astype(jnp.bfloat16), perm_ref[...], NT, preferred_element_type=jnp.float32
    )
    pot_ref[...] = moved[0:1, :] + moved[1:2, :] + moved[2:3, :]
    step = min(256, scaled_ref.shape[0])
    for i in range(0, scaled_ref.shape[0], step):
        plan = (scaled_ref[i : i + step, :] * w).astype(jnp.bfloat16)
        member_ref[:, i : i + step] = lax.dot_general(
            perm_ref[...], plan, NT, preferred_element_type=jnp.float32
        ).astype(member_ref.dtype)


def on_device(scenarios, rep_index):
    scen_rows, width = scenarios.shape
    n = lax.axis_size("scen")
    n_rep = lax.axis_size("rep")
    d = lax.axis_index("scen")
    rep = lax.axis_index("rep")
    count_r = rep_index.shape[0]
    count_s = scen_rows * n
    per = count_r // n
    features = width * n_rep
    rolled = per == LANES
    as_int = lambda x: x.astype(jnp.int32)

    ring = list(range(0, n, 2)) + list(range(n - 1, 0, -2))
    up = [(ring[i], ring[(i + 1) % n]) for i in range(n)]
    down = [(b, a) for a, b in up]
    place = jnp.where(d % 2 == 0, d // 2, n - 1 - d // 2)

    local = as_int(rep_index - d * scen_rows)
    i_scen = jnp.arange(scen_rows, dtype=jnp.int32)
    chosen = jnp.sum(as_int(local[:, None] == i_scen[None, :]), axis=0)
    before = jnp.sum(as_int((local[:, None] >= 0) & (local[:, None] < i_scen[None, :])), axis=0)
    key = jnp.where(chosen > 0, before, -1)
    sel = (key[None, :] == jnp.arange(per, dtype=jnp.int32)[:, None]).astype(scenarios.dtype)
    mine = pick(sel, scenarios)

    core = rep % 2
    ids = jnp.stack([core, place, (n - place) % n]).astype(jnp.int32)
    sq_scen = norms(scenarios)

    def swap(x, bit):
        return lax.ppermute(x, "rep", [(i, i ^ bit) for i in range(n_rep)])

    def total(chunks):
        send, keep = cost_share(ids, scenarios, sq_scen, chunks)
        part = keep + swap(send, 1)
        bit = 2
        while bit < n_rep:
            part = part + swap(part, bit)
            bit *= 2
        return part, swap(part, 1)

    halves = [mine[: per // 2], mine[per // 2 :]]
    a, b = halves, halves[::-1]
    stages = [total(halves)]
    slots = [[(0, 0)]]
    for k in range(1, n // 2 + 1):
        if k == n // 2:
            a, b = a[:1], b[:1]
        a = [lax.ppermute(c, "scen", up) for c in a]
        b = [lax.ppermute(c, "scen", down) for c in b]
        stages.append(total(a + b[::-1]))
    where = {0: (0, 0), n // 2: (n // 2, 0)}
    for k in range(1, n // 2):
        where[n - k], where[k] = (k, 0), (k, per)

    own, other = [s[0] for s in stages], [s[1] for s in stages]
    if not rolled:
        join = lambda xs: [
            jnp.concatenate([xs[where[q][0]][:, where[q][1] : where[q][1] + per] for q in range(n)], axis=1)
        ]
        own, other = join(own), join(other)
        pieces = [(0, i * LANES) for i in range(count_r // LANES)]
    else:
        pieces = [where[q] for q in range(n)]

    rows_out = count_r // n_rep
    wanted = lax.dynamic_slice_in_dim(rep_index, rep * rows_out, rows_out)
    rank = jnp.sum(as_int(rep_index[None, :] < wanted[:, None]), axis=1)
    block = rank // per
    slot = (jnp.where(block % 2 == 0, block // 2, n - 1 - block // 2) - place) % n
    at = slot * per + rank % per
    perm = (at[:, None] == jnp.arange(count_r, dtype=jnp.int32)[None, :]).astype(jnp.bfloat16)

    f32 = lambda *shape: jax.ShapeDtypeStruct(shape, jnp.float32)
    tiles = count_r // LANES
    sums = f32(n, tiles, LANES)

    def exchange(x):
        if not rolled:
            x = jnp.roll(x.reshape(n, count_r), place * per, axis=1).reshape(x.shape)
        x = lax.all_to_all(x, "scen", 0, 0, tiled=False)
        if not rolled:
            x = jnp.roll(x.reshape(n, count_r), -place * per, axis=1).reshape(x.shape)
        return x

    e, peak, x = pl.pallas_call(
        functools.partial(first_kernel, pieces=pieces, scale=-1.0 / (features * eps_blur), rolled=rolled),
        out_shape=(f32(scen_rows, count_r), f32(scen_rows, LANES), sums),
        in_specs=[SMEM] + [VMEM] * (2 * len(own)),
        out_specs=(VMEM,) * 3,
        name="first",
    )(ids, *own, *other)
    scale = count_s / count_r
    for _ in range(ITERS - 2):
        x = pl.pallas_call(
            functools.partial(step_kernel, scale=scale, rolled=rolled),
            out_shape=sums,
            in_specs=[SMEM, VMEM, VMEM],
            out_specs=VMEM,
            name="step",
        )(ids, exchange(x), e)
    x, scen_pot, scaled = pl.pallas_call(
        functools.partial(last_kernel, scale=scale, rolled=rolled, log_count=math.log(count_s)),
        out_shape=(sums, f32(scen_rows // LANES, LANES), f32(scen_rows, count_r)),
        in_specs=[SMEM] + [VMEM] * 3,
        out_specs=(VMEM,) * 3,
        scratch_shapes=[pltpu.VMEM((scen_rows, LANES), jnp.float32)],
        name="last",
    )(ids, exchange(x), e, peak)
    rep_pot, member = pl.pallas_call(
        functools.partial(out_kernel, scale=scale, rolled=rolled),
        out_shape=(f32(1, rows_out), jax.ShapeDtypeStruct((rows_out, scen_rows), jnp.bfloat16)),
        in_specs=[SMEM] + [VMEM] * 3,
        out_specs=(VMEM, VMEM),
        name="out",
    )(ids, exchange(x), scaled, perm)
    return scen_pot.reshape(scen_rows), rep_pot.reshape(rows_out), member


def solution(mesh):
    return jax.shard_map(
        on_device,
        mesh=mesh,
        in_specs=(P("scen", "rep"), P()),
        out_specs=(P("scen"), P("rep"), P("rep", "scen")),
        check_vma=False,
    )
```

```python
import functools
import math

import jax
import jax.numpy as jnp
from jax import lax
from jax.experimental import pallas as pl
from jax.experimental.pallas import tpu as pltpu
from jax.sharding import PartitionSpec as P

ITERS = 3
eps_blur = 0.1

LANES = 128
SUB = 8
NT = (((1,), (1,)), ((), ()))
VMEM = pl.BlockSpec(memory_space=pltpu.VMEM)
SMEM = pl.BlockSpec(memory_space=pltpu.SMEM)
ROOM = pltpu.CompilerParams(vmem_limit_bytes=10 * 2**20)


def kept(*xs):
    return [pltpu.with_memory_space_constraint(x, pltpu.VMEM) for x in xs]


def square_sums(x):
    gram = lax.dot_general(x, x, NT, preferred_element_type=jnp.float32)
    n = x.shape[0]
    eye = lax.broadcasted_iota(jnp.int32, (n, n), 0) == lax.broadcasted_iota(jnp.int32, (n, n), 1)
    return jnp.sum(jnp.where(eye, gram, 0.0), axis=0, keepdims=True)


def pick_kernel(sel_ref, scen_ref, low_ref, high_ref, *, step):
    half = low_ref.shape[0]
    for at in range(0, scen_ref.shape[1], step):
        cols = slice(at, at + step)
        rows = jnp.dot(sel_ref[...], scen_ref[:, cols], preferred_element_type=jnp.float32)
        low_ref[:, cols] = rows[:half].astype(low_ref.dtype)
        high_ref[:, cols] = rows[half:].astype(high_ref.dtype)


def pick(sel, scenarios):
    rows, width = sel.shape[0], scenarios.shape[1]
    return pl.pallas_call(
        functools.partial(pick_kernel, step=min(512, width)),
        out_shape=(pltpu.VMEM((rows // 2, width), scenarios.dtype),) * 2,
        in_specs=[VMEM] * 2,
        out_specs=(VMEM, VMEM),
        cost_estimate=pl.CostEstimate(
            flops=2 * rows * scenarios.size, bytes_accessed=2 * scenarios.size, transcendentals=0
        ),
        compiler_params=ROOM,
        name="pick",
    )(*kept(sel, scenarios))


def norm_kernel(scen_ref, out_ref):
    def body(i, carry):
        rows = pl.ds(pl.multiple_of(i * 16, 16), 16)
        x = scen_ref[rows, :].astype(jnp.float32)
        out_ref[rows, :] = jnp.broadcast_to(jnp.sum(x * x, axis=1, keepdims=True), (16, LANES))
        return carry

    lax.fori_loop(0, scen_ref.shape[0] // 16, body, 0, unroll=2)


def norms(scenarios):
    return pl.pallas_call(
        norm_kernel,
        out_shape=pltpu.VMEM((scenarios.shape[0], LANES), jnp.float32),
        in_specs=[VMEM],
        out_specs=VMEM,
        cost_estimate=pl.CostEstimate(
            flops=2 * scenarios.size, bytes_accessed=2 * scenarios.size, transcendentals=0
        ),
        compiler_params=ROOM,
        name="norms",
    )(*kept(scenarios))


def cost_kernel(core_ref, scen_ref, sq_ref, *refs, tile, merge):
    *refs, send_ref, keep_ref = refs
    chunks, before = (refs[:-2], refs[-2:]) if merge else (refs, (None, None))
    reps = jnp.concatenate([c[...] for c in chunks], axis=0)
    sq_rep = square_sums(reps)
    half = send_ref.shape[0]
    core = core_ref[0]
    cols = reps.shape[0]
    first = lax.broadcasted_iota(jnp.int32, (tile, cols), 1) < cols // 2
    for out_ref, old_ref, which in ((send_ref, before[0], 1 - core), (keep_ref, before[1], core)):
        for at in range(0, half, tile):
            rows = pl.ds(pl.multiple_of(which * half + at, tile), tile)
            cross = lax.dot_general(scen_ref[rows, :], reps, NT, preferred_element_type=jnp.float32)
            new = sq_rep + sq_ref[rows, 0:1] - 2.0 * cross
            if merge:
                old = old_ref[at : at + tile, :]
                out_ref[at : at + tile, :cols] = jnp.where(first, old, new)
                out_ref[at : at + tile, cols:] = jnp.where(first, new, old)
            else:
                out_ref[at : at + tile, :] = new


def cost_share(core, scenarios, sq_scen, chunks, before=()):
    rows, width = scenarios.shape
    cols = sum(c.shape[0] for c in chunks)
    half = pltpu.VMEM((rows // 2, cols * (2 if before else 1)), jnp.float32)
    return pl.pallas_call(
        functools.partial(cost_kernel, tile=min(256, rows // 2), merge=bool(before)),
        out_shape=(half, half),
        in_specs=[SMEM] + [VMEM] * (2 + len(chunks) + len(before)),
        out_specs=(VMEM, VMEM),
        cost_estimate=pl.CostEstimate(
            flops=2 * rows * cols * width, bytes_accessed=2 * rows * width, transcendentals=0
        ),
        compiler_params=ROOM,
        name="cost_share",
    )(core, *kept(scenarios, sq_scen, *chunks, *before))


def tree(op, xs):
    while len(xs) > 1:
        xs = [op(*xs[i : i + 2]) if i + 1 < len(xs) else xs[i] for i in range(0, len(xs), 2)]
    return xs[0]


def put_sums(acc, out_ref, shift):
    at = lax.broadcasted_iota(jnp.int32, (len(acc), LANES), 0)
    total = jnp.zeros((len(acc), LANES), jnp.float32)
    for i, a in enumerate(acc):
        total = jnp.where(at == i, jnp.sum(a, axis=0, keepdims=True), total)
    if shift is not None:
        total = pltpu.roll(total, shift, 0)
    for k in range(out_ref.shape[0]):
        out_ref[k] = total


def get_factors(got_ref, scale, shift):
    total = tree(jnp.add, [got_ref[k] for k in range(got_ref.shape[0])])
    if shift is not None:
        total = pltpu.roll(total, shift, 0)
    return scale / total


def spread(w):
    return [jnp.broadcast_to(w[i : i + 1, :], (SUB, LANES)) for i in range(w.shape[0])]


GROUP = 8


def load(ref, rows):
    return [ref[rows, k * LANES : (k + 1) * LANES] for k in range(ref.shape[1] // LANES)]


def store(ref, rows, tiles):
    for k, x in enumerate(tiles):
        ref[rows, k * LANES : (k + 1) * LANES] = x


def group_rows(i, g, base=0):
    return pl.ds(pl.multiple_of(base + (i * GROUP + g) * SUB, SUB), SUB)


def first_kernel(ids_ref, *refs, pieces, scale, rolled):
    stages = len(refs) // 2 - 1
    mine, other = refs[:stages], refs[stages : 2 * stages]
    e_ref, peak_ref, out_ref = refs[2 * stages :]
    half = mine[0].shape[0]
    core = ids_ref[0]
    left = lax.broadcasted_iota(jnp.int32, (SUB, LANES), 1) < LANES // 2

    def body(i, acc, h):
        peaks, sums = [], []
        for g in range(GROUP):
            src = group_rows(i, g)
            z = []
            for piece in pieces:
                part = [
                    jnp.where(core == h, mine[s][src, at : at + LANES], other[s][src, at : at + LANES])
                    for s, at in piece
                ]
                part = part[0] if len(part) == 1 else jnp.where(left, part[0], part[1])
                z.append(part * scale)
            store(e_ref, group_rows(i, g, h * half), z)
            peaks.append(tree(jnp.maximum, z))
        peaks = [jnp.max(p, axis=1, keepdims=True) for p in peaks]
        for g in range(GROUP):
            dst = group_rows(i, g, h * half)
            e = [jnp.exp2(x - peaks[g]) for x in load(e_ref, dst)]
            store(e_ref, dst, e)
            peak_ref[dst, :] = jnp.broadcast_to(peaks[g], (SUB, LANES))
            sums.append(tree(jnp.add, e))
        sums = [1.0 / jnp.sum(x, axis=1, keepdims=True) for x in sums]
        for g in range(GROUP):
            acc = [a + x * sums[g] for a, x in zip(acc, load(e_ref, group_rows(i, g, h * half)))]
        return tuple(acc)

    acc = tuple(jnp.zeros((SUB, LANES), jnp.float32) for _ in pieces)
    for h in range(2):
        acc = lax.fori_loop(0, half // (GROUP * SUB), functools.partial(body, h=h), acc)
    put_sums(acc, out_ref, ids_ref[1] if rolled else None)


def step_kernel(ids_ref, got_ref, e_ref, out_ref, *, scale, rolled):
    tiles = e_ref.shape[1] // LANES
    w = spread(get_factors(got_ref, scale, ids_ref[2] if rolled else None))

    def body(i, acc):
        sums = [tree(jnp.add, [x * f for x, f in zip(load(e_ref, group_rows(i, g)), w)]) for g in range(GROUP)]
        sums = [1.0 / jnp.sum(x, axis=1, keepdims=True) for x in sums]
        for g in range(GROUP):
            acc = [a + x * sums[g] for a, x in zip(acc, load(e_ref, group_rows(i, g)))]
        return tuple(acc)

    acc = tuple(jnp.zeros((SUB, LANES), jnp.float32) for _ in range(tiles))
    acc = lax.fori_loop(0, e_ref.shape[0] // (GROUP * SUB), body, acc)
    put_sums(acc, out_ref, ids_ref[1] if rolled else None)


def last_kernel(ids_ref, got_ref, e_ref, peak_ref, out_ref, pot_ref, scaled_ref, col_ref, *, scale, rolled, log_count):
    rows_all = e_ref.shape[0]
    tiles = e_ref.shape[1] // LANES
    w = spread(get_factors(got_ref, scale, ids_ref[2] if rolled else None))

    def body(i, acc):
        sums = [tree(jnp.add, [x * f for x, f in zip(load(e_ref, group_rows(i, g)), w)]) for g in range(GROUP)]
        sums = [jnp.sum(x, axis=1, keepdims=True) for x in sums]
        for g in range(GROUP):
            rows = group_rows(i, g)
            col_ref[rows, :] = -eps_blur * (log_count + math.log(2) * peak_ref[rows, :] + jnp.log(sums[g]))
            q = 1.0 / sums[g]
            e = [x * q for x in load(e_ref, rows)]
            store(scaled_ref, rows, e)
            acc = [a + x for a, x in zip(acc, e)]
        return tuple(acc)

    acc = tuple(jnp.zeros((SUB, LANES), jnp.float32) for _ in range(tiles))
    acc = lax.fori_loop(0, rows_all // (GROUP * SUB), body, acc)
    put_sums(acc, out_ref, ids_ref[1] if rolled else None)
    for i in range(rows_all // LANES):
        block = col_ref[i * LANES : (i + 1) * LANES, :]
        pot_ref[i : i + 1, :] = jnp.transpose(block)[0:1, :]


def out_kernel(ids_ref, got_ref, scaled_ref, perm_ref, pot_ref, member_ref, *, scale, rolled):
    tiles = scaled_ref.shape[1] // LANES
    factors = get_factors(got_ref, scale, ids_ref[2] if rolled else None)
    w = jnp.concatenate([factors[i : i + 1, :] for i in range(tiles)], axis=1)
    v = eps_blur * jnp.log(w)
    high = v.astype(jnp.bfloat16).astype(jnp.float32)
    mid = (v - high).astype(jnp.bfloat16).astype(jnp.float32)
    low = v - high - mid
    at = lax.broadcasted_iota(jnp.int32, (16, w.shape[1]), 0)
    parts = jnp.where(at == 0, high, jnp.where(at == 1, mid, jnp.where(at == 2, low, 0.0)))
    moved = lax.dot_general(
        parts.astype(jnp.bfloat16), perm_ref[...], NT, preferred_element_type=jnp.float32
    )
    pot_ref[...] = moved[0:1, :] + moved[1:2, :] + moved[2:3, :]
    step = min(256, scaled_ref.shape[0])
    for i in range(0, scaled_ref.shape[0], step):
        plan = (scaled_ref[i : i + step, :] * w).astype(jnp.bfloat16)
        member_ref[:, i : i + step] = lax.dot_general(
            perm_ref[...], plan, NT, preferred_element_type=jnp.float32
        ).astype(member_ref.dtype)


def on_device(scenarios, rep_index):
    scen_rows, width = scenarios.shape
    n = lax.axis_size("scen")
    n_rep = lax.axis_size("rep")
    count_r = rep_index.shape[0]
    count_s = scen_rows * n
    per = count_r // n
    features = width * n_rep
    rows_out = count_r // n_rep
    rolled = per == LANES
    as_int = lambda x: x.astype(jnp.int32)

    def tied(xs, *after):
        return list(lax.optimization_barrier((tuple(xs), after))[0])

    ring = list(range(0, n, 2)) + list(range(n - 1, 0, -2))
    up = [(ring[i], ring[(i + 1) % n]) for i in range(n)]
    down = [(b, a) for a, b in up]
    at_ring = [ring.index(i) for i in range(n)]

    d = lax.axis_index("scen")
    rep = lax.axis_index("rep")
    place = jnp.where((d & 1) == 0, d >> 1, n - 1 - (d >> 1))
    back = jnp.where(place == 0, 0, n - place)
    scalars = tuple(x.astype(jnp.int32) for x in (rep & 1, place, back, d * scen_rows, rep * rows_out))
    rep_index, *scalars = tied([rep_index, *scalars])
    core, place, back, scen_from, out_from = scalars
    ids = jnp.stack([core, place, back])
    wanted = lax.dynamic_slice_in_dim(rep_index, out_from, rows_out)
    rep_index, ids, wanted, place, scen_from = tied([rep_index, ids, wanted, place, scen_from])

    local = rep_index - scen_from
    i_scen = jnp.arange(scen_rows, dtype=jnp.int32)
    chosen = jnp.sum(as_int(local[:, None] == i_scen[None, :]), axis=0)
    before = jnp.sum(as_int((local[:, None] >= 0) & (local[:, None] < i_scen[None, :])), axis=0)
    key = jnp.where(chosen > 0, before, -1)
    sel = (key[None, :] == jnp.arange(per, dtype=jnp.int32)[:, None]).astype(scenarios.dtype)
    halves = list(pick(sel, scenarios))

    rank = jnp.sum(as_int(rep_index[None, :] < wanted[:, None]), axis=1)
    block = rank // per
    at = sum(jnp.where(block == i, at_ring[i], 0) for i in range(n)) - place
    at = jnp.where(at < 0, at + n, at) * per + rank % per
    perm = (at[:, None] == jnp.arange(count_r, dtype=jnp.int32)[None, :]).astype(jnp.bfloat16)

    def swap(x, bit):
        return lax.ppermute(x, "rep", [(i, i ^ bit) for i in range(n_rep)])

    def rest(part):
        bit = 2
        while bit < n_rep:
            part = part + swap(part, bit)
            bit *= 2
        return part

    stages = []
    where = [None] * n

    def finish(send, keep):
        part = keep + swap(send, 1)
        whole = rest(part)
        other = swap(whole, 1)
        stages.append((whole, other))
        return part, whole, other

    sq_scen = norms(scenarios)
    shares = cost_share(ids, scenarios, sq_scen, halves)
    ties = {1: [*shares, perm], 2: [], 3: [], 4: []}
    part, whole, other = finish(*shares)
    ties[2] += [part]
    ties[4] += [whole]
    where[0] = [(0, 0)]
    a, b = halves, halves[::-1]
    for h in range(1, n):
        i, k = (h + 1) % 2, (h + 1) // 2
        x = lax.ppermute(a[i], "scen", up)
        y = lax.ppermute(b[i], "scen", down)
        x, y = tied([x, y], *ties.pop(h, []))
        if i == 0:
            a, b = [x, a[1]], [y, b[1]]
            shares = cost_share(ids, scenarios, sq_scen, [x, y])
        else:
            a, b = [a[0], x], [b[0], y]
            joined = h < n - 3
            shares = cost_share(ids, scenarios, sq_scen, [y, x], shares if joined else ())
        ties.setdefault(h + 1, []).extend(shares)
        if i == 1 or h >= n - 3:
            part, whole, other = finish(*shares)
            ties.setdefault(h + 2, []).append(part)
            ties.setdefault(h + 4, []).append(whole)
            ties.setdefault(h + 5, []).append(other)
            s = len(stages) - 1
            if h == n - 1:
                where[k] = [(s, 0)]
            elif i == 1 and h < n - 3:
                where[n - k], where[k] = [(s, 0)], [(s, per)]
            elif i == 1:
                where[n - k], where[k] = [(s - 1, 0), (s, 0)], [(s, 0), (s - 1, 0)]

    own, other = [s[0] for s in stages], [s[1] for s in stages]
    if not rolled:

        def join(xs):
            cols = []
            for piece in where:
                part = [xs[s][:, at : at + per] for s, at in piece]
                cols += part if len(part) == 1 else [part[0][:, : per // 2], part[1][:, per // 2 :]]
            return [jnp.concatenate(cols, axis=1)]

        own, other = join(own), join(other)
        pieces = [[(0, i * LANES)] for i in range(count_r // LANES)]
    else:
        pieces = where

    f32 = lambda *shape: pltpu.VMEM(shape, jnp.float32)
    tiles = count_r // LANES
    sums = f32(n, tiles, LANES)

    def exchange(x):
        if not rolled:
            x = jnp.roll(x.reshape(n, count_r), place * per, axis=1).reshape(x.shape)
        x = lax.all_to_all(x, "scen", 0, 0, tiled=False)
        if not rolled:
            x = jnp.roll(x.reshape(n, count_r), -place * per, axis=1).reshape(x.shape)
        return x

    e, peak, x = pl.pallas_call(
        functools.partial(first_kernel, pieces=pieces, scale=-1.0 / (features * eps_blur * math.log(2)), rolled=rolled),
        out_shape=(f32(scen_rows, count_r), f32(scen_rows, LANES), sums),
        in_specs=[SMEM] + [VMEM] * (2 * len(own)),
        out_specs=(VMEM,) * 3,
        compiler_params=ROOM,
        name="first",
    )(ids, *kept(*own, *other))
    scale = count_s / count_r
    for _ in range(ITERS - 2):
        x = pl.pallas_call(
            functools.partial(step_kernel, scale=scale, rolled=rolled),
            out_shape=sums,
            in_specs=[SMEM, VMEM, VMEM],
            out_specs=VMEM,
            compiler_params=ROOM,
            name="step",
        )(ids, *kept(exchange(x), e))
    x, scen_pot, scaled = pl.pallas_call(
        functools.partial(last_kernel, scale=scale, rolled=rolled, log_count=math.log(count_s)),
        out_shape=(
            sums,
            jax.ShapeDtypeStruct((scen_rows // LANES, LANES), jnp.float32),
            f32(scen_rows, count_r),
        ),
        in_specs=[SMEM] + [VMEM] * 3,
        out_specs=(VMEM,) * 3,
        scratch_shapes=[pltpu.VMEM((scen_rows, LANES), jnp.float32)],
        compiler_params=ROOM,
        name="last",
    )(ids, *kept(exchange(x), e, peak))
    rep_pot, member = pl.pallas_call(
        functools.partial(out_kernel, scale=scale, rolled=rolled),
        out_shape=(
            jax.ShapeDtypeStruct((1, rows_out), jnp.float32),
            jax.ShapeDtypeStruct((rows_out, scen_rows), jnp.bfloat16),
        ),
        in_specs=[SMEM] + [VMEM] * 3,
        out_specs=(VMEM, VMEM),
        compiler_params=ROOM,
        name="out",
    )(ids, *kept(exchange(x), scaled, perm))
    return scen_pot.reshape(scen_rows), rep_pot.reshape(rows_out), member


def solution(mesh):
    return jax.shard_map(
        on_device,
        mesh=mesh,
        in_specs=(P("scen", "rep"), P()),
        out_specs=(P("scen"), P("rep"), P("rep", "scen")),
        check_vma=False,
    )
```

```python
import functools
import math

import jax
import jax.numpy as jnp
from jax import lax
from jax.experimental import pallas as pl
from jax.experimental.pallas import tpu as pltpu
from jax.sharding import PartitionSpec as P

ITERS = 3
eps_blur = 0.1

LANES = 128
SUB = 8
NT = (((1,), (1,)), ((), ()))
VMEM = pl.BlockSpec(memory_space=pltpu.VMEM)
SMEM = pl.BlockSpec(memory_space=pltpu.SMEM)
AFTER = {0: (2, 3, 4), 5: (2, 0, 4), 4: (1, 2, 3), 3: (1, 0, 0), 2: (1, 0, 0), 1: (0, 0, 0)}
COST = pl.CostEstimate(flops=4 * 10**9, bytes_accessed=10**7, transcendentals=0)
ROOM = pltpu.CompilerParams(vmem_limit_bytes=10 * 2**20)


def kept(*xs):
    return [pltpu.with_memory_space_constraint(x, pltpu.VMEM) for x in xs]


def square_sums(x):
    gram = lax.dot_general(x, x, NT, preferred_element_type=jnp.float32)
    n = x.shape[0]
    eye = lax.broadcasted_iota(jnp.int32, (n, n), 0) == lax.broadcasted_iota(jnp.int32, (n, n), 1)
    return jnp.sum(jnp.where(eye, gram, 0.0), axis=0, keepdims=True)


def pick_kernel(index_ref, scen_ref, kept_ref, low_ref, high_ref, col_ref, sel_ref, sems, *, step):
    rows_all, width = scen_ref.shape
    copies = [
        pltpu.make_async_copy(scen_ref.at[:, at : at + step], kept_ref.at[:, at : at + step], sems.at[i])
        for i, at in enumerate(range(0, width, step))
    ]
    for copy in copies:
        copy.start()
    local = index_ref[...] - lax.axis_index("scen") * rows_all
    local = jnp.where(local >= 0, local, 2 * rows_all)
    tiles = [jnp.broadcast_to(local[i : i + 1, :], (SUB, LANES)) for i in range(local.shape[0])]
    sub = lax.broadcasted_iota(jnp.int32, (SUB, LANES), 0)
    lane = lax.broadcasted_iota(jnp.int32, (SUB, LANES), 1).astype(jnp.float32)

    def body(i, carry):
        keys = []
        for g in range(16):
            row = sub + (i * 16 + g) * SUB
            hits = [jnp.where(t == row, 4096.0, jnp.where(t < row, 1.0, 0.0)) for t in tiles]
            keys.append(tree(jnp.add, hits))
        keys = [jnp.sum(x, axis=1, keepdims=True) for x in keys]
        for g in range(16):
            rows = pl.ds(pl.multiple_of((i * 16 + g) * SUB, SUB), SUB)
            col_ref[rows, :] = jnp.where(lane == keys[g] - 4096.0, 1.0, 0.0)
        return carry

    lax.fori_loop(0, rows_all // LANES, body, 0)
    per = 2 * low_ref.shape[0]
    for at in range(0, rows_all, LANES):
        block = jnp.transpose(col_ref[at : at + LANES, :])
        sel_ref[:, at : at + LANES] = block[:per].astype(sel_ref.dtype)
    for i, at in enumerate(range(0, width, step)):
        copies[i].wait()
        cols = slice(at, at + step)
        rows = jnp.dot(sel_ref[...], kept_ref[:, cols], preferred_element_type=jnp.float32)
        low_ref[:, cols] = rows[: per // 2].astype(low_ref.dtype)
        high_ref[:, cols] = rows[per // 2 :].astype(high_ref.dtype)


def pick(rep_index, scenarios, per):
    rows, width = scenarios.shape
    step = min(512, width)
    some = pltpu.VMEM((per // 2, width), scenarios.dtype)
    return pl.pallas_call(
        functools.partial(pick_kernel, step=step),
        out_shape=(pltpu.VMEM((rows, width), scenarios.dtype), some, some),
        in_specs=[VMEM, pl.BlockSpec(memory_space=pltpu.HBM)],
        out_specs=(VMEM,) * 3,
        scratch_shapes=[
            pltpu.VMEM((rows, LANES), jnp.float32),
            pltpu.VMEM((per, rows), scenarios.dtype),
            pltpu.SemaphoreType.DMA((width // step,)),
        ],
        cost_estimate=COST,
        compiler_params=ROOM,
        name="pick",
    )(rep_index.reshape(-1, LANES), pltpu.with_memory_space_constraint(scenarios, pltpu.HBM))


def norm_kernel(scen_ref, out_ref):
    def body(i, carry):
        rows = pl.ds(pl.multiple_of(i * 16, 16), 16)
        x = scen_ref[rows, :].astype(jnp.float32)
        out_ref[rows, :] = jnp.broadcast_to(jnp.sum(x * x, axis=1, keepdims=True), (16, LANES))
        return carry

    lax.fori_loop(0, scen_ref.shape[0] // 16, body, 0, unroll=2)


def norms(scenarios):
    return pl.pallas_call(
        norm_kernel,
        out_shape=pltpu.VMEM((scenarios.shape[0], LANES), jnp.float32),
        in_specs=[VMEM],
        out_specs=VMEM,
        cost_estimate=COST,
        compiler_params=ROOM,
        name="norms",
    )(*kept(scenarios))


def cost_kernel(core_ref, scen_ref, sq_ref, *refs, tile, parts):
    chunks, outs = refs[: -len(parts)], refs[-len(parts) :]
    reps = jnp.concatenate([c[...] for c in chunks], axis=0)
    sq_rep = square_sums(reps)
    half = outs[0].shape[0]
    for flip, out_ref in zip(parts, outs, strict=True):
        which = 1 - core_ref[0] if flip else core_ref[0]
        for at in range(0, half, tile):
            rows = pl.ds(pl.multiple_of(which * half + at, tile), tile)
            cross = lax.dot_general(scen_ref[rows, :], reps, NT, preferred_element_type=jnp.float32)
            out_ref[at : at + tile, :] = sq_rep + sq_ref[rows, 0:1] - 2.0 * cross


def cost_share(core, scenarios, sq_scen, chunks, parts=(True, False)):
    rows, width = scenarios.shape
    half = pltpu.VMEM((rows // 2, sum(c.shape[0] for c in chunks)), jnp.float32)
    return pl.pallas_call(
        functools.partial(cost_kernel, tile=min(256, rows // 2), parts=parts),
        out_shape=(half,) * len(parts),
        in_specs=[SMEM] + [VMEM] * (2 + len(chunks)),
        out_specs=(VMEM,) * len(parts),
        cost_estimate=COST,
        compiler_params=ROOM,
        name="cost_share",
    )(core, *kept(scenarios, sq_scen, *chunks))


def tree(op, xs):
    while len(xs) > 1:
        xs = [op(*xs[i : i + 2]) if i + 1 < len(xs) else xs[i] for i in range(0, len(xs), 2)]
    return xs[0]


def put_sums(acc, out_ref, shift):
    at = lax.broadcasted_iota(jnp.int32, (len(acc), LANES), 0)
    total = jnp.zeros((len(acc), LANES), jnp.float32)
    for i, a in enumerate(acc):
        total = jnp.where(at == i, jnp.sum(a, axis=0, keepdims=True), total)
    if shift is not None:
        total = pltpu.roll(total, shift, 0)
    for k in range(out_ref.shape[0]):
        out_ref[k] = total


def get_factors(got_ref, scale, shift):
    total = tree(jnp.add, [got_ref[k] for k in range(got_ref.shape[0])])
    if shift is not None:
        total = pltpu.roll(total, shift, 0)
    return scale / total


def spread(w):
    return [jnp.broadcast_to(w[i : i + 1, :], (SUB, LANES)) for i in range(w.shape[0])]


GROUP = 16


def load(ref, rows):
    return [ref[rows, k * LANES : (k + 1) * LANES] for k in range(ref.shape[1] // LANES)]


def store(ref, rows, tiles):
    for k, x in enumerate(tiles):
        ref[rows, k * LANES : (k + 1) * LANES] = x


def group_rows(i, g, base=0):
    return pl.ds(pl.multiple_of(base + (i * GROUP + g) * SUB, SUB), SUB)


def cost_tiles(refs, pieces, src, here, left, scale):
    mine, other = refs[: len(refs) // 2], refs[len(refs) // 2 :]
    tiles = []
    for piece in pieces:
        part = [
            jnp.where(here, mine[s][src, at : at + LANES], other[s][src, at : at + LANES])
            for s, at in piece
        ]
        part = part[0] if len(part) == 1 else jnp.where(left, part[0], part[1])
        tiles.append(part * scale)
    return tiles


def early_kernel(ids_ref, *refs, pieces, scale):
    *refs, e_ref, peak_ref, sum_ref = refs
    half = refs[0].shape[0]
    left = lax.broadcasted_iota(jnp.int32, (SUB, LANES), 1) < LANES // 2

    def body(i, carry, h):
        peaks, sums = [], []
        for g in range(GROUP):
            z = cost_tiles(refs, pieces, group_rows(i, g), ids_ref[0] == h, left, scale)
            store(e_ref, group_rows(i, g, h * half), z)
            peaks.append(tree(jnp.maximum, z))
        peaks = [jnp.max(p, axis=1, keepdims=True) for p in peaks]
        for g in range(GROUP):
            dst = group_rows(i, g, h * half)
            e = [jnp.exp2(x - peaks[g]) for x in load(e_ref, dst)]
            store(e_ref, dst, e)
            peak_ref[dst, :] = jnp.broadcast_to(peaks[g], (SUB, LANES))
            sums.append(tree(jnp.add, e))
        for g in range(GROUP):
            total = jnp.sum(sums[g], axis=1, keepdims=True)
            sum_ref[group_rows(i, g, h * half), :] = jnp.broadcast_to(total, (SUB, LANES))
        return carry

    for h in range(2):
        lax.fori_loop(0, half // (GROUP * SUB), functools.partial(body, h=h), 0)


def late_kernel(ids_ref, early_ref, old_peak_ref, old_sum_ref, *refs, pieces, order, scale, rolled):
    *refs, e_ref, peak_ref, out_ref = refs
    half = refs[0].shape[0]
    left = lax.broadcasted_iota(jnp.int32, (SUB, LANES), 1) < LANES // 2
    early = early_ref.shape[1] // LANES
    at = [slice(k * LANES, (k + 1) * LANES) for k in order]

    def body(i, acc, h):
        peaks, sums, factors = [], [], []
        for g in range(GROUP):
            dst = group_rows(i, g, h * half)
            z = cost_tiles(refs, pieces, group_rows(i, g), ids_ref[0] == h, left, scale)
            for k, x in zip(at[early:], z, strict=True):
                e_ref[dst, k] = x
            peaks.append(tree(jnp.maximum, z))
        peaks = [jnp.max(p, axis=1, keepdims=True) for p in peaks]
        for g in range(GROUP):
            dst = group_rows(i, g, h * half)
            peak = jnp.maximum(old_peak_ref[dst, :], peaks[g])
            factor = jnp.exp2(old_peak_ref[dst, :] - peak)
            peak_ref[dst, :] = peak
            factors.append(factor)
            e = [jnp.exp2(e_ref[dst, k] - peak) for k in at[early:]]
            for k, x in zip(at[early:], e, strict=True):
                e_ref[dst, k] = x
            sums.append(tree(jnp.add, e))
        sums = [jnp.sum(x, axis=1, keepdims=True) for x in sums]
        for g in range(GROUP):
            dst = group_rows(i, g, h * half)
            q = 1.0 / (old_sum_ref[dst, :] * factors[g] + sums[g])
            e = [x * factors[g] for x in load(early_ref, dst)]
            for k, x in zip(at[:early], e, strict=True):
                e_ref[dst, k] = x
            e += [e_ref[dst, k] for k in at[early:]]
            acc = [a + x * q for a, x in zip(acc, e, strict=True)]
        return tuple(acc)

    acc = tuple(jnp.zeros((SUB, LANES), jnp.float32) for _ in order)
    for h in range(2):
        acc = lax.fori_loop(0, half // (GROUP * SUB), functools.partial(body, h=h), acc)
    acc = [acc[order.index(k)] for k in range(len(order))]
    put_sums(acc, out_ref, ids_ref[1] if rolled else None)


def step_kernel(ids_ref, got_ref, e_ref, out_ref, *, scale, rolled):
    tiles = e_ref.shape[1] // LANES
    w = spread(get_factors(got_ref, scale, ids_ref[2] if rolled else None))

    def body(i, acc):
        sums = [tree(jnp.add, [x * f for x, f in zip(load(e_ref, group_rows(i, g)), w)]) for g in range(GROUP)]
        sums = [1.0 / jnp.sum(x, axis=1, keepdims=True) for x in sums]
        for g in range(GROUP):
            acc = [a + x * sums[g] for a, x in zip(acc, load(e_ref, group_rows(i, g)))]
        return tuple(acc)

    acc = tuple(jnp.zeros((SUB, LANES), jnp.float32) for _ in range(tiles))
    acc = lax.fori_loop(0, e_ref.shape[0] // (GROUP * SUB), body, acc)
    put_sums(acc, out_ref, ids_ref[1] if rolled else None)


def last_kernel(ids_ref, got_ref, e_ref, peak_ref, out_ref, pot_ref, scaled_ref, col_ref, *, scale, rolled, log_count):
    rows_all = e_ref.shape[0]
    tiles = e_ref.shape[1] // LANES
    w = spread(get_factors(got_ref, scale, ids_ref[2] if rolled else None))

    def body(i, acc):
        sums = [tree(jnp.add, [x * f for x, f in zip(load(e_ref, group_rows(i, g)), w)]) for g in range(GROUP)]
        sums = [jnp.sum(x, axis=1, keepdims=True) for x in sums]
        for g in range(GROUP):
            rows = group_rows(i, g)
            col_ref[rows, :] = -eps_blur * (log_count + math.log(2) * peak_ref[rows, :] + jnp.log(sums[g]))
            q = 1.0 / sums[g]
            e = [x * q for x in load(e_ref, rows)]
            store(scaled_ref, rows, e)
            acc = [a + x for a, x in zip(acc, e)]
        return tuple(acc)

    acc = tuple(jnp.zeros((SUB, LANES), jnp.float32) for _ in range(tiles))
    acc = lax.fori_loop(0, rows_all // (GROUP * SUB), body, acc)
    put_sums(acc, out_ref, ids_ref[1] if rolled else None)
    shape = (LANES, LANES)
    eye = lax.broadcasted_iota(jnp.int32, shape, 0) == lax.broadcasted_iota(jnp.int32, shape, 1)
    for i in range(rows_all // LANES):
        block = col_ref[i * LANES : (i + 1) * LANES, :]
        pot_ref[i : i + 1, :] = jnp.sum(jnp.where(eye, block, 0.0), axis=0, keepdims=True)


def out_kernel(ids_ref, got_ref, scaled_ref, perm_ref, pot_ref, member_ref, *, scale, rolled):
    tiles = scaled_ref.shape[1] // LANES
    factors = get_factors(got_ref, scale, ids_ref[2] if rolled else None)
    w = jnp.concatenate([factors[i : i + 1, :] for i in range(tiles)], axis=1)
    v = eps_blur * jnp.log(w)
    high = v.astype(jnp.bfloat16).astype(jnp.float32)
    mid = (v - high).astype(jnp.bfloat16).astype(jnp.float32)
    low = v - high - mid
    at = lax.broadcasted_iota(jnp.int32, (16, w.shape[1]), 0)
    parts = jnp.where(at == 0, high, jnp.where(at == 1, mid, jnp.where(at == 2, low, 0.0)))
    moved = lax.dot_general(
        parts.astype(jnp.bfloat16), perm_ref[...], NT, preferred_element_type=jnp.float32
    )
    pot_ref[...] = moved[0:1, :] + moved[1:2, :] + moved[2:3, :]
    step = min(256, scaled_ref.shape[0])
    for i in range(0, scaled_ref.shape[0], step):
        plan = (scaled_ref[i : i + step, :] * w).astype(jnp.bfloat16)
        member_ref[:, i : i + step] = lax.dot_general(
            perm_ref[...], plan, NT, preferred_element_type=jnp.float32
        ).astype(member_ref.dtype)


def on_device(scenarios, rep_index):
    scen_rows, width = scenarios.shape
    n = lax.axis_size("scen")
    n_rep = lax.axis_size("rep")
    count_r = rep_index.shape[0]
    count_s = scen_rows * n
    per = count_r // n
    features = width * n_rep
    rows_out = count_r // n_rep
    rolled = per == LANES
    as_int = lambda x: x.astype(jnp.int32)

    def tied(xs, *after):
        return list(lax.optimization_barrier((tuple(xs), after))[0])

    ring = list(range(0, n, 2)) + list(range(n - 1, 0, -2))
    up = [(ring[i], ring[(i + 1) % n]) for i in range(n)]
    down = [(b, a) for a, b in up]
    at_ring = [ring.index(i) for i in range(n)]

    d = lax.axis_index("scen")
    rep = lax.axis_index("rep")
    place = jnp.where((d & 1) == 0, d >> 1, n - 1 - (d >> 1))
    back = jnp.where(place == 0, 0, n - place)
    scalars = tuple(x.astype(jnp.int32) for x in (rep & 1, place, back, rep * rows_out))
    rep_index, core, place, back, out_from = tied([rep_index, *scalars])

    scenarios, *halves = pick(rep_index, scenarios, per)
    ids = jnp.stack([core, place, back])
    wanted = lax.dynamic_slice(rep_index, (out_from,), (rows_out,), allow_negative_indices=False)

    rank = jnp.sum(as_int(rep_index[None, :] < wanted[:, None]), axis=1)
    block = rank // per
    at = sum(jnp.where(block == i, at_ring[i], 0) for i in range(n)) - place
    at = jnp.where(at < 0, at + n, at) * per + rank % per
    perm = (at[:, None] == jnp.arange(count_r, dtype=jnp.int32)[None, :]).astype(jnp.bfloat16)

    def swap(x, bit):
        return lax.ppermute(x, "rep", [(i, i ^ bit) for i in range(n_rep)])

    def rest(part, *after):
        bit = 2
        while bit < n_rep:
            got = swap(part, bit)
            if after:
                (got,) = tied([got], *after)
            part = part + got
            bit *= 2
        return part

    stages = []
    where = [None] * n

    def finish(part, *after):
        whole = rest(part, *after)
        other = swap(whole, 1)
        stages.append((whole, other))
        return whole, other

    f32 = lambda *shape: pltpu.VMEM(shape, jnp.float32)
    tiles = count_r // LANES
    to_power = -1.0 / (features * eps_blur * math.log(2))

    def start_early(pieces, stages):
        given = [s[0] for s in stages] + [s[1] for s in stages]
        return pl.pallas_call(
            functools.partial(early_kernel, pieces=pieces, scale=to_power),
            out_shape=(f32(scen_rows, len(pieces) * LANES), f32(scen_rows, LANES), f32(scen_rows, LANES)),
            in_specs=[SMEM] + [VMEM] * len(given),
            out_specs=(VMEM,) * 3,
            cost_estimate=COST,
            compiler_params=ROOM,
            name="early",
        )(ids, *kept(*given))

    ties = {}

    def tie(h, after, *xs):
        if after:
            ties.setdefault(h + after, []).extend(xs)

    sq_scen = norms(scenarios)
    shares = cost_share(ids, scenarios, sq_scen, halves)
    tie(0, 1, perm)
    a, b = halves, halves[::-1]
    a[1], b[1] = tied([a[1], b[1]], sq_scen)
    begun = []
    for h in range(n):
        i, k = (h + 1) % 2, (h + 1) // 2
        if h:
            a[i], b[i] = (lax.ppermute(x, "scen", way) for x, way in ((a[i], up), (b[i], down)))
            a[i], b[i] = tied([a[i], b[i]], *ties.pop(h, []))
            chunks = [b[i], a[i]] if i else [a[i], b[i]]
        if h == n - 1:
            sent = cost_share(ids, scenarios, sq_scen, chunks, parts=(True,))
            finish(part, *sent, *begun)
            shares = [*sent, *cost_share(ids, scenarios, sq_scen, chunks, parts=(False,))]
        elif h:
            shares = cost_share(ids, scenarios, sq_scen, chunks)
        part = shares[1] + swap(shares[0], 1)
        after = AFTER.get(n - h, AFTER[0])
        tie(h, 1, *shares)
        tie(h, after[0], part)
        if h != n - 2:
            whole, other = finish(part)
            tie(h, after[1], whole)
            tie(h, after[2], other)
        if h in (0, n - 1):
            where[k] = [(h, 0)]
        elif i == 1:
            where[n - k], where[k] = [(h - 1, 0), (h, 0)], [(h, 0), (h - 1, 0)]
        if rolled and h == n - 4:
            begun = start_early([w for w in where if w], stages)

    own, other = [s[0] for s in stages], [s[1] for s in stages]
    if rolled:
        cut = len(stages) - 3
        order = sorted(range(n), key=lambda q: where[q][0][0] >= cut)
        pieces = [[(s - cut, at) for s, at in where[q]] for q in order if where[q][0][0] >= cut]
        late = own[cut:] + other[cut:]
    else:

        def join(xs):
            cols = []
            for piece in where:
                part = [xs[s][:, at : at + per] for s, at in piece]
                cols += part if len(part) == 1 else [part[0][:, : per // 2], part[1][:, per // 2 :]]
            return jnp.concatenate(cols, axis=1)

        order = list(range(tiles))
        pieces = [[(0, i * LANES)] for i in order]
        late = [join(own), join(other)]
        begun = start_early(pieces[: tiles // 2], [late])
        pieces = pieces[tiles // 2 :]

    sums = f32(n, tiles, LANES)

    def exchange(x):
        if not rolled:
            x = jnp.roll(x.reshape(n, count_r), place * per, axis=1).reshape(x.shape)
        x = lax.all_to_all(x, "scen", 0, 0, tiled=False)
        if not rolled:
            x = jnp.roll(x.reshape(n, count_r), -place * per, axis=1).reshape(x.shape)
        return x

    e, peak, x = pl.pallas_call(
        functools.partial(late_kernel, pieces=pieces, order=order, scale=to_power, rolled=rolled),
        out_shape=(f32(scen_rows, count_r), f32(scen_rows, LANES), sums),
        in_specs=[SMEM] + [VMEM] * (3 + len(late)),
        out_specs=(VMEM,) * 3,
        compiler_params=ROOM,
        name="late",
    )(ids, *kept(*begun, *late))
    scale = count_s / count_r
    for _ in range(ITERS - 2):
        x = pl.pallas_call(
            functools.partial(step_kernel, scale=scale, rolled=rolled),
            out_shape=sums,
            in_specs=[SMEM, VMEM, VMEM],
            out_specs=VMEM,
            compiler_params=ROOM,
            name="step",
        )(ids, *kept(exchange(x), e))
    x, scen_pot, scaled = pl.pallas_call(
        functools.partial(last_kernel, scale=scale, rolled=rolled, log_count=math.log(count_s)),
        out_shape=(
            sums,
            jax.ShapeDtypeStruct((scen_rows // LANES, LANES), jnp.float32),
            f32(scen_rows, count_r),
        ),
        in_specs=[SMEM] + [VMEM] * 3,
        out_specs=(VMEM,) * 3,
        scratch_shapes=[pltpu.VMEM((scen_rows, LANES), jnp.float32)],
        compiler_params=ROOM,
        name="last",
    )(ids, *kept(exchange(x), e, peak))
    rep_pot, member = pl.pallas_call(
        functools.partial(out_kernel, scale=scale, rolled=rolled),
        out_shape=(
            jax.ShapeDtypeStruct((1, rows_out), jnp.float32),
            jax.ShapeDtypeStruct((rows_out, scen_rows), jnp.bfloat16),
        ),
        in_specs=[SMEM] + [VMEM] * 3,
        out_specs=(VMEM, VMEM),
        compiler_params=ROOM,
        name="out",
    )(ids, *kept(exchange(x), scaled, perm))
    return scen_pot.reshape(scen_rows), rep_pot.reshape(rows_out), member


def solution(mesh):
    return jax.shard_map(
        on_device,
        mesh=mesh,
        in_specs=(P("scen", "rep"), P()),
        out_specs=(P("scen"), P("rep"), P("rep", "scen")),
        check_vma=False,
    )
```

```python
import functools
import math

import jax
import jax.numpy as jnp
from jax import lax
from jax.experimental import pallas as pl
from jax.experimental.pallas import tpu as pltpu
from jax.sharding import PartitionSpec as P

ITERS = 3
eps_blur = 0.1

LANES = 128
SUB = 8
NT = (((1,), (1,)), ((), ()))
VMEM = pl.BlockSpec(memory_space=pltpu.VMEM)
SMEM = pl.BlockSpec(memory_space=pltpu.SMEM)
AFTER = {0: (2, 3, 4), 5: (2, 0, 4), 4: (1, 2, 3), 3: (1, 2, 0), 2: (1, 0, 0), 1: (0, 0, 0)}
COST = pl.CostEstimate(flops=4 * 10**9, bytes_accessed=10**7, transcendentals=0)
ROOM = pltpu.CompilerParams(vmem_limit_bytes=10 * 2**20)


def kept(*xs):
    return [pltpu.with_memory_space_constraint(x, pltpu.VMEM) for x in xs]


def square_sums(chunks):
    sums = []
    for c in chunks:
        x = c[...].astype(jnp.float32)
        sums.append(jnp.sum(x * x, axis=1, keepdims=True))
    column = jnp.concatenate(sums, axis=0)
    n = column.shape[0]
    eye = lax.broadcasted_iota(jnp.int32, (n, n), 0) == lax.broadcasted_iota(jnp.int32, (n, n), 1)
    return jnp.sum(jnp.where(eye, column, 0.0), axis=0, keepdims=True)


def pick_kernel(index_hbm, scen_ref, kept_ref, low_ref, high_ref, index_ref, col_ref, sel_ref, sems, *, step):
    rows_all, width = scen_ref.shape
    copies = [
        pltpu.make_async_copy(scen_ref.at[:, at : at + step], kept_ref.at[:, at : at + step], sems.at[i])
        for i, at in enumerate(range(0, width, step))
    ]
    fetch = pltpu.make_async_copy(index_hbm, index_ref, sems.at[len(copies)])
    fetch.start()
    for copy in copies:
        copy.start()
    fetch.wait()
    local = index_ref[...] - lax.axis_index("scen") * rows_all
    local = jnp.where(local >= 0, local, 2 * rows_all)
    tiles = [jnp.broadcast_to(local[i : i + 1, :], (SUB, LANES)) for i in range(local.shape[0])]
    sub = lax.broadcasted_iota(jnp.int32, (SUB, LANES), 0)
    lane = lax.broadcasted_iota(jnp.int32, (SUB, LANES), 1).astype(jnp.float32)

    def body(i, carry):
        keys = []
        for g in range(16):
            row = sub + (i * 16 + g) * SUB
            hits = [jnp.where(t == row, 4096.0, jnp.where(t < row, 1.0, 0.0)) for t in tiles]
            keys.append(tree(jnp.add, hits))
        keys = [jnp.sum(x, axis=1, keepdims=True) for x in keys]
        for g in range(16):
            rows = pl.ds(pl.multiple_of((i * 16 + g) * SUB, SUB), SUB)
            col_ref[rows, :] = jnp.where(lane == keys[g] - 4096.0, 1.0, 0.0)
        return carry

    lax.fori_loop(0, rows_all // LANES, body, 0)
    per = 2 * low_ref.shape[0]
    for at in range(0, rows_all, LANES):
        block = jnp.transpose(col_ref[at : at + LANES, :])
        sel_ref[:, at : at + LANES] = block[:per].astype(sel_ref.dtype)
    for i, at in enumerate(range(0, width, step)):
        copies[i].wait()
        cols = slice(at, at + step)
        rows = jnp.dot(sel_ref[...], kept_ref[:, cols], preferred_element_type=jnp.float32)
        low_ref[:, cols] = rows[: per // 2].astype(low_ref.dtype)
        high_ref[:, cols] = rows[per // 2 :].astype(high_ref.dtype)


def pick(rep_index, scenarios, per):
    rows, width = scenarios.shape
    step = min(1024, width)
    some = pltpu.VMEM((per // 2, width), scenarios.dtype)
    return pl.pallas_call(
        functools.partial(pick_kernel, step=step),
        out_shape=(pltpu.VMEM((rows, width), scenarios.dtype), some, some),
        in_specs=[pl.BlockSpec(memory_space=pltpu.HBM)] * 2,
        out_specs=(VMEM,) * 3,
        scratch_shapes=[
            pltpu.VMEM((rep_index.size // LANES, LANES), rep_index.dtype),
            pltpu.VMEM((rows, LANES), jnp.float32),
            pltpu.VMEM((per, rows), scenarios.dtype),
            pltpu.SemaphoreType.DMA((width // step + 1,)),
        ],
        cost_estimate=COST,
        compiler_params=ROOM,
        name="pick",
    )(*(pltpu.with_memory_space_constraint(x, pltpu.HBM) for x in (rep_index.reshape(-1, LANES), scenarios)))


def norm_kernel(scen_ref, out_ref):
    def body(i, carry):
        rows = pl.ds(pl.multiple_of(i * 16, 16), 16)
        x = scen_ref[rows, :].astype(jnp.float32)
        out_ref[rows, :] = jnp.broadcast_to(jnp.sum(x * x, axis=1, keepdims=True), (16, LANES))
        return carry

    lax.fori_loop(0, scen_ref.shape[0] // 16, body, 0, unroll=2)


def norms(scenarios):
    return pl.pallas_call(
        norm_kernel,
        out_shape=pltpu.VMEM((scenarios.shape[0], LANES), jnp.float32),
        in_specs=[VMEM],
        out_specs=VMEM,
        cost_estimate=COST,
        compiler_params=ROOM,
        name="norms",
    )(*kept(scenarios))


def cost_kernel(core_ref, scen_ref, sq_ref, *refs, tile, parts):
    chunks, outs = refs[: -len(parts)], refs[-len(parts) :]
    reps = jnp.concatenate([c[...] for c in chunks], axis=0)
    sq_rep = square_sums(chunks)
    half = outs[0].shape[0]
    for flip, out_ref in zip(parts, outs, strict=True):
        which = 1 - core_ref[0] if flip else core_ref[0]
        for at in range(0, half, tile):
            rows = pl.ds(pl.multiple_of(which * half + at, tile), tile)
            cross = lax.dot_general(scen_ref[rows, :], reps, NT, preferred_element_type=jnp.float32)
            out_ref[at : at + tile, :] = sq_rep + sq_ref[rows, 0:1] - 2.0 * cross


def cost_share(core, scenarios, sq_scen, chunks, parts=(True, False)):
    rows, width = scenarios.shape
    half = pltpu.VMEM((rows // 2, sum(c.shape[0] for c in chunks)), jnp.float32)
    return pl.pallas_call(
        functools.partial(cost_kernel, tile=min(256, rows // 2), parts=parts),
        out_shape=(half,) * len(parts),
        in_specs=[SMEM] + [VMEM] * (2 + len(chunks)),
        out_specs=(VMEM,) * len(parts),
        cost_estimate=COST,
        compiler_params=ROOM,
        name="cost_share",
    )(core, *kept(scenarios, sq_scen, *chunks))


def tree(op, xs):
    while len(xs) > 1:
        xs = [op(*xs[i : i + 2]) if i + 1 < len(xs) else xs[i] for i in range(0, len(xs), 2)]
    return xs[0]


def put_sums(acc, out_ref, shift):
    at = lax.broadcasted_iota(jnp.int32, (len(acc), LANES), 0)
    total = jnp.zeros((len(acc), LANES), jnp.float32)
    for i, a in enumerate(acc):
        total = jnp.where(at == i, jnp.sum(a, axis=0, keepdims=True), total)
    if shift is not None:
        total = pltpu.roll(total, shift, 0)
    for k in range(out_ref.shape[0]):
        out_ref[k] = total


def get_factors(got_ref, scale, shift):
    total = tree(jnp.add, [got_ref[k] for k in range(got_ref.shape[0])])
    if shift is not None:
        total = pltpu.roll(total, shift, 0)
    return scale / total


def spread(w):
    return [jnp.broadcast_to(w[i : i + 1, :], (SUB, LANES)) for i in range(w.shape[0])]


def group_of(rows):
    return math.gcd(64, rows // SUB)


def load(ref, rows):
    return [ref[rows, k * LANES : (k + 1) * LANES] for k in range(ref.shape[1] // LANES)]


def store(ref, rows, tiles):
    for k, x in enumerate(tiles):
        ref[rows, k * LANES : (k + 1) * LANES] = x


def group_rows(i, g, group, base=0):
    return pl.ds(pl.multiple_of(base + (i * group + g) * SUB, SUB), SUB)


def cost_tiles(refs, pieces, src, here, left, scale):
    mine, other = refs[: len(refs) // 2], refs[len(refs) // 2 :]
    tiles = []
    for piece in pieces:
        part = [
            jnp.where(here, mine[s][src, at : at + LANES], other[s][src, at : at + LANES])
            for s, at in piece
        ]
        part = part[0] if len(part) == 1 else jnp.where(left, part[0], part[1])
        tiles.append(part * scale)
    return tiles


def early_kernel(ids_ref, *refs, pieces, scale):
    *refs, e_ref, peak_ref, sum_ref = refs
    half = refs[0].shape[0]
    left = lax.broadcasted_iota(jnp.int32, (SUB, LANES), 1) < LANES // 2
    group = group_of(half)

    def body(i, carry, h):
        peaks, sums = [], []
        for g in range(group):
            z = cost_tiles(refs, pieces, group_rows(i, g, group), ids_ref[0] == h, left, scale)
            store(e_ref, group_rows(i, g, group, h * half), z)
            peaks.append(tree(jnp.maximum, z))
        peaks = [jnp.max(p, axis=1, keepdims=True) for p in peaks]
        for g in range(group):
            dst = group_rows(i, g, group, h * half)
            e = [jnp.exp2(x - peaks[g]) for x in load(e_ref, dst)]
            store(e_ref, dst, e)
            peak_ref[dst, :] = jnp.broadcast_to(peaks[g], (SUB, LANES))
            sums.append(tree(jnp.add, e))
        for g in range(group):
            total = jnp.sum(sums[g], axis=1, keepdims=True)
            sum_ref[group_rows(i, g, group, h * half), :] = jnp.broadcast_to(total, (SUB, LANES))
        return carry

    for h in range(2):
        lax.fori_loop(0, half // (group * SUB), functools.partial(body, h=h), 0)


def late_kernel(ids_ref, early_ref, old_peak_ref, old_sum_ref, *refs, pieces, order, scale, rolled):
    *refs, e_ref, peak_ref, out_ref = refs
    half = refs[0].shape[0]
    left = lax.broadcasted_iota(jnp.int32, (SUB, LANES), 1) < LANES // 2
    group = group_of(half)
    early = early_ref.shape[1] // LANES
    at = [slice(k * LANES, (k + 1) * LANES) for k in order]

    def body(i, acc, h):
        peaks, sums, factors = [], [], []
        for g in range(group):
            dst = group_rows(i, g, group, h * half)
            z = cost_tiles(refs, pieces, group_rows(i, g, group), ids_ref[0] == h, left, scale)
            for k, x in zip(at[early:], z, strict=True):
                e_ref[dst, k] = x
            peaks.append(tree(jnp.maximum, z))
        peaks = [jnp.max(p, axis=1, keepdims=True) for p in peaks]
        for g in range(group):
            dst = group_rows(i, g, group, h * half)
            peak = jnp.maximum(old_peak_ref[dst, :], peaks[g])
            factor = jnp.exp2(old_peak_ref[dst, :] - peak)
            peak_ref[dst, :] = peak
            factors.append(factor)
            e = [jnp.exp2(e_ref[dst, k] - peak) for k in at[early:]]
            for k, x in zip(at[early:], e, strict=True):
                e_ref[dst, k] = x
            sums.append(tree(jnp.add, e))
        sums = [jnp.sum(x, axis=1, keepdims=True) for x in sums]
        for g in range(group):
            dst = group_rows(i, g, group, h * half)
            q = 1.0 / (old_sum_ref[dst, :] * factors[g] + sums[g])
            e = [x * factors[g] for x in load(early_ref, dst)]
            for k, x in zip(at[:early], e, strict=True):
                e_ref[dst, k] = x
            e += [e_ref[dst, k] for k in at[early:]]
            acc = [a + x * q for a, x in zip(acc, e, strict=True)]
        return tuple(acc)

    acc = tuple(jnp.zeros((SUB, LANES), jnp.float32) for _ in order)
    for h in range(2):
        acc = lax.fori_loop(0, half // (group * SUB), functools.partial(body, h=h), acc)
    acc = [acc[order.index(k)] for k in range(len(order))]
    put_sums(acc, out_ref, ids_ref[1] if rolled else None)


def step_kernel(ids_ref, got_ref, e_ref, out_ref, *, scale, rolled):
    tiles = e_ref.shape[1] // LANES
    group = group_of(e_ref.shape[0])
    w = spread(get_factors(got_ref, scale, ids_ref[2] if rolled else None))

    def body(i, acc):
        sums = [tree(jnp.add, [x * f for x, f in zip(load(e_ref, group_rows(i, g, group)), w)]) for g in range(group)]
        sums = [1.0 / jnp.sum(x, axis=1, keepdims=True) for x in sums]
        for g in range(group):
            acc = [a + x * sums[g] for a, x in zip(acc, load(e_ref, group_rows(i, g, group)))]
        return tuple(acc)

    acc = tuple(jnp.zeros((SUB, LANES), jnp.float32) for _ in range(tiles))
    acc = lax.fori_loop(0, e_ref.shape[0] // (group * SUB), body, acc)
    put_sums(acc, out_ref, ids_ref[1] if rolled else None)


def last_kernel(ids_ref, got_ref, e_ref, peak_ref, out_ref, pot_ref, scaled_ref, col_ref, *, scale, rolled, log_count):
    rows_all = e_ref.shape[0]
    tiles = e_ref.shape[1] // LANES
    group = group_of(e_ref.shape[0])
    w = spread(get_factors(got_ref, scale, ids_ref[2] if rolled else None))

    def body(i, acc):
        sums = [tree(jnp.add, [x * f for x, f in zip(load(e_ref, group_rows(i, g, group)), w)]) for g in range(group)]
        sums = [jnp.sum(x, axis=1, keepdims=True) for x in sums]
        for g in range(group):
            rows = group_rows(i, g, group)
            col_ref[rows, :] = -eps_blur * (log_count + math.log(2) * peak_ref[rows, :] + jnp.log(sums[g]))
            q = 1.0 / sums[g]
            e = [x * q for x in load(e_ref, rows)]
            store(scaled_ref, rows, e)
            acc = [a + x for a, x in zip(acc, e)]
        return tuple(acc)

    acc = tuple(jnp.zeros((SUB, LANES), jnp.float32) for _ in range(tiles))
    acc = lax.fori_loop(0, rows_all // (group * SUB), body, acc)
    put_sums(acc, out_ref, ids_ref[1] if rolled else None)
    shape = (LANES, LANES)
    eye = lax.broadcasted_iota(jnp.int32, shape, 0) == lax.broadcasted_iota(jnp.int32, shape, 1)
    for i in range(rows_all // LANES):
        block = col_ref[i * LANES : (i + 1) * LANES, :]
        pot_ref[i : i + 1, :] = jnp.sum(jnp.where(eye, block, 0.0), axis=0, keepdims=True)


def out_kernel(ids_ref, got_ref, scaled_ref, perm_ref, pot_ref, member_ref, *, scale, rolled):
    tiles = scaled_ref.shape[1] // LANES
    factors = get_factors(got_ref, scale, ids_ref[2] if rolled else None)
    w = jnp.concatenate([factors[i : i + 1, :] for i in range(tiles)], axis=1)
    v = eps_blur * jnp.log(w)
    high = v.astype(jnp.bfloat16).astype(jnp.float32)
    mid = (v - high).astype(jnp.bfloat16).astype(jnp.float32)
    low = v - high - mid
    at = lax.broadcasted_iota(jnp.int32, (16, w.shape[1]), 0)
    parts = jnp.where(at == 0, high, jnp.where(at == 1, mid, jnp.where(at == 2, low, 0.0)))
    moved = lax.dot_general(
        parts.astype(jnp.bfloat16), perm_ref[...], NT, preferred_element_type=jnp.float32
    )
    pot_ref[...] = moved[0:1, :] + moved[1:2, :] + moved[2:3, :]
    step = min(256, scaled_ref.shape[0])
    for i in range(0, scaled_ref.shape[0], step):
        plan = (scaled_ref[i : i + step, :] * w).astype(jnp.bfloat16)
        member_ref[:, i : i + step] = lax.dot_general(
            perm_ref[...], plan, NT, preferred_element_type=jnp.float32
        ).astype(member_ref.dtype)


def on_device(scenarios, rep_index):
    scen_rows, width = scenarios.shape
    n = lax.axis_size("scen")
    n_rep = lax.axis_size("rep")
    count_r = rep_index.shape[0]
    count_s = scen_rows * n
    per = count_r // n
    features = width * n_rep
    rows_out = count_r // n_rep
    rolled = per == LANES
    as_int = lambda x: x.astype(jnp.int32)

    def tied(xs, *after):
        return list(lax.optimization_barrier((tuple(xs), after))[0])

    ring = list(range(0, n, 2)) + list(range(n - 1, 0, -2))
    up = [(ring[i], ring[(i + 1) % n]) for i in range(n)]
    down = [(b, a) for a, b in up]
    at_ring = [ring.index(i) for i in range(n)]

    d = lax.axis_index("scen")
    rep = lax.axis_index("rep")
    place = jnp.where((d & 1) == 0, d >> 1, n - 1 - (d >> 1))
    back = jnp.where(place == 0, 0, n - place)
    scalars = tuple(x.astype(jnp.int32) for x in (rep & 1, place, back, rep * rows_out))
    rep_index, core, place, back, out_from = tied([rep_index, *scalars])

    scenarios, *halves = pick(rep_index, scenarios, per)
    ids = jnp.stack([core, place, back])
    wanted = lax.dynamic_slice(rep_index, (out_from,), (rows_out,), allow_negative_indices=False)

    rank = jnp.sum(as_int(rep_index[None, :] < wanted[:, None]), axis=1)
    block = rank // per
    at = sum(jnp.where(block == i, at_ring[i], 0) for i in range(n)) - place
    at = jnp.where(at < 0, at + n, at) * per + rank % per
    perm = (at[:, None] == jnp.arange(count_r, dtype=jnp.int32)[None, :]).astype(jnp.bfloat16)

    def swap(x, bit):
        return lax.ppermute(x, "rep", [(i, i ^ bit) for i in range(n_rep)])

    def rest(part, *after):
        bit = 2
        while bit < n_rep:
            got = swap(part, bit)
            if after:
                (got,) = tied([got], *after)
            part = part + got
            bit *= 2
        return part

    stages = []
    where = [None] * n

    def finish(part, *after):
        whole = rest(part, *after)
        other = swap(whole, 1)
        stages.append((whole, other))
        return whole, other

    f32 = lambda *shape: pltpu.VMEM(shape, jnp.float32)
    tiles = count_r // LANES
    to_power = -1.0 / (features * eps_blur * math.log(2))

    def start_early(pieces, stages):
        given = [s[0] for s in stages] + [s[1] for s in stages]
        return pl.pallas_call(
            functools.partial(early_kernel, pieces=pieces, scale=to_power),
            out_shape=(f32(scen_rows, len(pieces) * LANES), f32(scen_rows, LANES), f32(scen_rows, LANES)),
            in_specs=[SMEM] + [VMEM] * len(given),
            out_specs=(VMEM,) * 3,
            cost_estimate=COST,
            compiler_params=ROOM,
            name="early",
        )(ids, *kept(*given))

    ties = {}

    def tie(h, after, *xs):
        if after:
            ties.setdefault(h + after, []).extend(xs)

    sq_scen = norms(scenarios)
    shares = cost_share(ids, scenarios, sq_scen, halves)
    tie(0, 1, perm)
    a, b = halves, halves[::-1]
    a[1], b[1] = tied([a[1], b[1]], sq_scen)
    waiting = []
    for h in range(n):
        i, k = (h + 1) % 2, (h + 1) // 2
        if h:
            a[i], b[i] = (lax.ppermute(x, "scen", way) for x, way in ((a[i], up), (b[i], down)))
            a[i], b[i] = tied([a[i], b[i]], *ties.pop(h, []))
            chunks = [b[i], a[i]] if i else [a[i], b[i]]
        if h == n - 1:
            sent = cost_share(ids, scenarios, sq_scen, chunks, parts=(True,))
            shares = [*sent, *cost_share(ids, scenarios, sq_scen, chunks, parts=(False,))]
        elif h:
            sent = shares = cost_share(ids, scenarios, sq_scen, chunks)
        for g, part in waiting:
            whole, other = finish(part, *sent, *(begun if g == n - 2 else ()))
            tie(g, AFTER[n - g][1], whole)
            tie(g, AFTER[n - g][2], other)
        waiting = []
        part = shares[1] + swap(shares[0], 1)
        after = AFTER.get(n - h, AFTER[0])
        tie(h, 1, *shares)
        tie(h, after[0], part)
        if h in (n - 3, n - 2):
            waiting.append((h, part))
        else:
            whole, other = finish(part)
            tie(h, after[1], whole)
            tie(h, after[2], other)
        if h in (0, n - 1):
            where[k] = [(h, 0)]
        elif i == 1:
            where[n - k], where[k] = [(h - 1, 0), (h, 0)], [(h, 0), (h - 1, 0)]
        if h == n - 4:
            begun = start_early([w for w in where if w], stages) if rolled else ()

    own, other = [s[0] for s in stages], [s[1] for s in stages]
    if rolled:
        cut = len(stages) - 3
        order = sorted(range(n), key=lambda q: where[q][0][0] >= cut)
        pieces = [[(s - cut, at) for s, at in where[q]] for q in order if where[q][0][0] >= cut]
        late = own[cut:] + other[cut:]
    else:

        def join(xs):
            cols = []
            for piece in where:
                part = [xs[s][:, at : at + per] for s, at in piece]
                cols += part if len(part) == 1 else [part[0][:, : per // 2], part[1][:, per // 2 :]]
            return jnp.concatenate(cols, axis=1)

        order = list(range(tiles))
        pieces = [[(0, i * LANES)] for i in order]
        late = [join(own), join(other)]
        begun = start_early(pieces[: tiles // 2], [late])
        pieces = pieces[tiles // 2 :]

    sums = f32(n, tiles, LANES)

    def exchange(x):
        if not rolled:
            x = jnp.roll(x.reshape(n, count_r), place * per, axis=1).reshape(x.shape)
        x = lax.all_to_all(x, "scen", 0, 0, tiled=False)
        if not rolled:
            x = jnp.roll(x.reshape(n, count_r), -place * per, axis=1).reshape(x.shape)
        return x

    e, peak, x = pl.pallas_call(
        functools.partial(late_kernel, pieces=pieces, order=order, scale=to_power, rolled=rolled),
        out_shape=(f32(scen_rows, count_r), f32(scen_rows, LANES), sums),
        in_specs=[SMEM] + [VMEM] * (3 + len(late)),
        out_specs=(VMEM,) * 3,
        compiler_params=ROOM,
        name="late",
    )(ids, *kept(*begun, *late))
    scale = count_s / count_r
    for _ in range(ITERS - 2):
        x = pl.pallas_call(
            functools.partial(step_kernel, scale=scale, rolled=rolled),
            out_shape=sums,
            in_specs=[SMEM, VMEM, VMEM],
            out_specs=VMEM,
            compiler_params=ROOM,
            name="step",
        )(ids, *kept(exchange(x), e))
    x, scen_pot, scaled = pl.pallas_call(
        functools.partial(last_kernel, scale=scale, rolled=rolled, log_count=math.log(count_s)),
        out_shape=(
            sums,
            jax.ShapeDtypeStruct((scen_rows // LANES, LANES), jnp.float32),
            f32(scen_rows, count_r),
        ),
        in_specs=[SMEM] + [VMEM] * 3,
        out_specs=(VMEM,) * 3,
        scratch_shapes=[pltpu.VMEM((scen_rows, LANES), jnp.float32)],
        compiler_params=ROOM,
        name="last",
    )(ids, *kept(exchange(x), e, peak))
    rep_pot, member = pl.pallas_call(
        functools.partial(out_kernel, scale=scale, rolled=rolled),
        out_shape=(
            jax.ShapeDtypeStruct((1, rows_out), jnp.float32),
            jax.ShapeDtypeStruct((rows_out, scen_rows), jnp.bfloat16),
        ),
        in_specs=[SMEM] + [VMEM] * 3,
        out_specs=(VMEM, VMEM),
        compiler_params=ROOM,
        name="out",
    )(ids, *kept(exchange(x), scaled, perm))
    return scen_pot.reshape(scen_rows), rep_pot.reshape(rows_out), member


def solution(mesh):
    return jax.shard_map(
        on_device,
        mesh=mesh,
        in_specs=(P("scen", "rep"), P()),
        out_specs=(P("scen"), P("rep"), P("rep", "scen")),
        check_vma=False,
    )
```

```python
import functools
import math

import jax
import jax.numpy as jnp
from jax import lax
from jax.experimental import pallas as pl
from jax.experimental.pallas import tpu as pltpu
from jax.sharding import PartitionSpec as P

ITERS = 3
eps_blur = 0.1

LANES = 128
SUB = 8
NT = (((1,), (1,)), ((), ()))
VMEM = pl.BlockSpec(memory_space=pltpu.VMEM)
SMEM = pl.BlockSpec(memory_space=pltpu.SMEM)
AFTER = {0: (2, 3, 4), 5: (2, 0, 4), 4: (1, 2, 3), 3: (1, 2, 0), 2: (1, 0, 0), 1: (0, 0, 0)}
COST = pl.CostEstimate(flops=4 * 10**9, bytes_accessed=10**7, transcendentals=0)
ROOM = pltpu.CompilerParams(vmem_limit_bytes=10 * 2**20)


def kept(*xs):
    return [pltpu.with_memory_space_constraint(x, pltpu.VMEM) for x in xs]


def square_sums(chunks):
    sums = []
    for c in chunks:
        x = c[...].astype(jnp.float32)
        sums.append(jnp.sum(x * x, axis=1, keepdims=True))
    column = jnp.concatenate(sums, axis=0)
    n = column.shape[0]
    eye = lax.broadcasted_iota(jnp.int32, (n, n), 0) == lax.broadcasted_iota(jnp.int32, (n, n), 1)
    return jnp.sum(jnp.where(eye, column, 0.0), axis=0, keepdims=True)


def pick_kernel(index_hbm, scen_ref, kept_ref, low_ref, high_ref, index_ref, col_ref, sel_ref, sems, *, step):
    rows_all, width = scen_ref.shape
    copies = [
        pltpu.make_async_copy(scen_ref.at[:, at : at + step], kept_ref.at[:, at : at + step], sems.at[i])
        for i, at in enumerate(range(0, width, step))
    ]
    fetch = pltpu.make_async_copy(index_hbm, index_ref, sems.at[len(copies)])
    fetch.start()
    for copy in copies:
        copy.start()
    fetch.wait()
    local = index_ref[...] - lax.axis_index("scen") * rows_all
    local = jnp.where(local >= 0, local, 2 * rows_all)
    tiles = [jnp.broadcast_to(local[i : i + 1, :], (SUB, LANES)) for i in range(local.shape[0])]
    sub = lax.broadcasted_iota(jnp.int32, (SUB, LANES), 0)
    lane = lax.broadcasted_iota(jnp.int32, (SUB, LANES), 1).astype(jnp.float32)

    def body(i, carry):
        keys = []
        for g in range(16):
            row = sub + (i * 16 + g) * SUB
            hits = [jnp.where(t == row, 4096.0, jnp.where(t < row, 1.0, 0.0)) for t in tiles]
            keys.append(tree(jnp.add, hits))
        keys = [jnp.sum(x, axis=1, keepdims=True) for x in keys]
        for g in range(16):
            rows = pl.ds(pl.multiple_of((i * 16 + g) * SUB, SUB), SUB)
            col_ref[rows, :] = jnp.where(lane == keys[g] - 4096.0, 1.0, 0.0)
        return carry

    lax.fori_loop(0, rows_all // LANES, body, 0)
    per = 2 * low_ref.shape[0]
    for at in range(0, rows_all, LANES):
        block = jnp.transpose(col_ref[at : at + LANES, :])
        sel_ref[:, at : at + LANES] = block[:per].astype(sel_ref.dtype)
    for i, at in enumerate(range(0, width, step)):
        copies[i].wait()
        cols = slice(at, at + step)
        rows = jnp.dot(sel_ref[...], kept_ref[:, cols], preferred_element_type=jnp.float32)
        low_ref[:, cols] = rows[: per // 2].astype(low_ref.dtype)
        high_ref[:, cols] = rows[per // 2 :].astype(high_ref.dtype)


def pick(rep_index, scenarios, per):
    rows, width = scenarios.shape
    step = min(1024, width)
    some = pltpu.VMEM((per // 2, width), scenarios.dtype)
    return pl.pallas_call(
        functools.partial(pick_kernel, step=step),
        out_shape=(pltpu.VMEM((rows, width), scenarios.dtype), some, some),
        in_specs=[pl.BlockSpec(memory_space=pltpu.HBM)] * 2,
        out_specs=(VMEM,) * 3,
        scratch_shapes=[
            pltpu.VMEM((rep_index.size // LANES, LANES), rep_index.dtype),
            pltpu.VMEM((rows, LANES), jnp.float32),
            pltpu.VMEM((per, rows), scenarios.dtype),
            pltpu.SemaphoreType.DMA((width // step + 1,)),
        ],
        cost_estimate=COST,
        compiler_params=ROOM,
        name="pick",
    )(*(pltpu.with_memory_space_constraint(x, pltpu.HBM) for x in (rep_index.reshape(-1, LANES), scenarios)))


def norm_kernel(scen_ref, out_ref):
    def body(i, carry):
        rows = pl.ds(pl.multiple_of(i * 16, 16), 16)
        x = scen_ref[rows, :].astype(jnp.float32)
        out_ref[rows, :] = jnp.broadcast_to(jnp.sum(x * x, axis=1, keepdims=True), (16, LANES))
        return carry

    lax.fori_loop(0, scen_ref.shape[0] // 16, body, 0, unroll=2)


def norms(scenarios):
    return pl.pallas_call(
        norm_kernel,
        out_shape=pltpu.VMEM((scenarios.shape[0], LANES), jnp.float32),
        in_specs=[VMEM],
        out_specs=VMEM,
        cost_estimate=COST,
        compiler_params=ROOM,
        name="norms",
    )(*kept(scenarios))


def cost_kernel(core_ref, scen_ref, sq_ref, *refs, tile, parts):
    chunks, outs = refs[: -len(parts)], refs[-len(parts) :]
    reps = jnp.concatenate([c[...] for c in chunks], axis=0)
    sq_rep = square_sums(chunks)
    half = outs[0].shape[0]
    for flip, out_ref in zip(parts, outs, strict=True):
        which = 1 - core_ref[0] if flip else core_ref[0]
        for at in range(0, half, tile):
            rows = pl.ds(pl.multiple_of(which * half + at, tile), tile)
            cross = lax.dot_general(scen_ref[rows, :], reps, NT, preferred_element_type=jnp.float32)
            out_ref[at : at + tile, :] = sq_rep + sq_ref[rows, 0:1] - 2.0 * cross


def cost_share(core, scenarios, sq_scen, chunks, parts=(True, False)):
    rows, width = scenarios.shape
    half = pltpu.VMEM((rows // 2, sum(c.shape[0] for c in chunks)), jnp.float32)
    return pl.pallas_call(
        functools.partial(cost_kernel, tile=min(256, rows // 2), parts=parts),
        out_shape=(half,) * len(parts),
        in_specs=[SMEM] + [VMEM] * (2 + len(chunks)),
        out_specs=(VMEM,) * len(parts),
        cost_estimate=COST,
        compiler_params=ROOM,
        name="cost_share",
    )(core, *kept(scenarios, sq_scen, *chunks))


def tree(op, xs):
    while len(xs) > 1:
        xs = [op(*xs[i : i + 2]) if i + 1 < len(xs) else xs[i] for i in range(0, len(xs), 2)]
    return xs[0]


def put_sums(acc, out_ref, shift):
    at = lax.broadcasted_iota(jnp.int32, (len(acc), LANES), 0)
    total = jnp.zeros((len(acc), LANES), jnp.float32)
    for i, a in enumerate(acc):
        total = jnp.where(at == i, jnp.sum(a, axis=0, keepdims=True), total)
    if shift is not None:
        total = pltpu.roll(total, shift, 0)
    for k in range(out_ref.shape[0]):
        out_ref[k] = total


def get_factors(got_ref, scale, shift):
    total = tree(jnp.add, [got_ref[k] for k in range(got_ref.shape[0])])
    if shift is not None:
        total = pltpu.roll(total, shift, 0)
    return scale / total


def spread(w):
    return [jnp.broadcast_to(w[i : i + 1, :], (SUB, LANES)) for i in range(w.shape[0])]


def group_of(rows):
    return math.gcd(64, rows // SUB)


def load(ref, rows):
    return [ref[rows, k * LANES : (k + 1) * LANES] for k in range(ref.shape[1] // LANES)]


def store(ref, rows, tiles):
    for k, x in enumerate(tiles):
        ref[rows, k * LANES : (k + 1) * LANES] = x


def group_rows(i, g, group, base=0):
    return pl.ds(pl.multiple_of(base + (i * group + g) * SUB, SUB), SUB)


def cost_tiles(refs, pieces, src, here, left, scale):
    mine, other = refs[: len(refs) // 2], refs[len(refs) // 2 :]
    tiles = []
    for piece in pieces:
        part = [
            jnp.where(here, mine[s][src, at : at + LANES], other[s][src, at : at + LANES])
            for s, at in piece
        ]
        part = part[0] if len(part) == 1 else jnp.where(left, part[0], part[1])
        tiles.append(part * scale)
    return tiles


def early_kernel(ids_ref, *refs, pieces, scale):
    *refs, e_ref, peak_ref, sum_ref = refs
    half = refs[0].shape[0]
    left = lax.broadcasted_iota(jnp.int32, (SUB, LANES), 1) < LANES // 2
    group = group_of(half)

    def body(i, carry, h):
        peaks, sums = [], []
        for g in range(group):
            z = cost_tiles(refs, pieces, group_rows(i, g, group), ids_ref[0] == h, left, scale)
            store(e_ref, group_rows(i, g, group, h * half), z)
            peaks.append(tree(jnp.maximum, z))
        peaks = [jnp.max(p, axis=1, keepdims=True) for p in peaks]
        for g in range(group):
            dst = group_rows(i, g, group, h * half)
            e = [jnp.exp2(x - peaks[g]) for x in load(e_ref, dst)]
            store(e_ref, dst, e)
            peak_ref[dst, :] = jnp.broadcast_to(peaks[g], (SUB, LANES))
            sums.append(tree(jnp.add, e))
        for g in range(group):
            total = jnp.sum(sums[g], axis=1, keepdims=True)
            sum_ref[group_rows(i, g, group, h * half), :] = jnp.broadcast_to(total, (SUB, LANES))
        return carry

    for h in range(2):
        lax.fori_loop(0, half // (group * SUB), functools.partial(body, h=h), 0)


def late_kernel(ids_ref, early_ref, old_peak_ref, old_sum_ref, *refs, pieces, order, scale, rolled):
    *refs, e_ref, peak_ref, out_ref = refs
    half = refs[0].shape[0]
    left = lax.broadcasted_iota(jnp.int32, (SUB, LANES), 1) < LANES // 2
    group = group_of(half)
    early = early_ref.shape[1] // LANES
    at = [slice(k * LANES, (k + 1) * LANES) for k in order]

    def body(i, acc, h):
        peaks, sums, factors = [], [], []
        for g in range(group):
            dst = group_rows(i, g, group, h * half)
            z = cost_tiles(refs, pieces, group_rows(i, g, group), ids_ref[0] == h, left, scale)
            for k, x in zip(at[early:], z, strict=True):
                e_ref[dst, k] = x
            peaks.append(tree(jnp.maximum, z))
        peaks = [jnp.max(p, axis=1, keepdims=True) for p in peaks]
        for g in range(group):
            dst = group_rows(i, g, group, h * half)
            peak = jnp.maximum(old_peak_ref[dst, :], peaks[g])
            factor = jnp.exp2(old_peak_ref[dst, :] - peak)
            peak_ref[dst, :] = peak
            factors.append(factor)
            e = [jnp.exp2(e_ref[dst, k] - peak) for k in at[early:]]
            for k, x in zip(at[early:], e, strict=True):
                e_ref[dst, k] = x
            sums.append(tree(jnp.add, e))
        sums = [jnp.sum(x, axis=1, keepdims=True) for x in sums]
        for g in range(group):
            dst = group_rows(i, g, group, h * half)
            q = 1.0 / (old_sum_ref[dst, :] * factors[g] + sums[g])
            e = [x * factors[g] for x in load(early_ref, dst)]
            for k, x in zip(at[:early], e, strict=True):
                e_ref[dst, k] = x
            e += [e_ref[dst, k] for k in at[early:]]
            acc = [a + x * q for a, x in zip(acc, e, strict=True)]
        return tuple(acc)

    acc = tuple(jnp.zeros((SUB, LANES), jnp.float32) for _ in order)
    for h in range(2):
        acc = lax.fori_loop(0, half // (group * SUB), functools.partial(body, h=h), acc)
    acc = [acc[order.index(k)] for k in range(len(order))]
    put_sums(acc, out_ref, ids_ref[1] if rolled else None)


def step_kernel(ids_ref, got_ref, e_ref, out_ref, *, scale, rolled):
    tiles = e_ref.shape[1] // LANES
    group = group_of(e_ref.shape[0])
    w = spread(get_factors(got_ref, scale, ids_ref[2] if rolled else None))

    def body(i, acc):
        sums = [tree(jnp.add, [x * f for x, f in zip(load(e_ref, group_rows(i, g, group)), w)]) for g in range(group)]
        sums = [1.0 / jnp.sum(x, axis=1, keepdims=True) for x in sums]
        for g in range(group):
            acc = [a + x * sums[g] for a, x in zip(acc, load(e_ref, group_rows(i, g, group)))]
        return tuple(acc)

    acc = tuple(jnp.zeros((SUB, LANES), jnp.float32) for _ in range(tiles))
    acc = lax.fori_loop(0, e_ref.shape[0] // (group * SUB), body, acc)
    put_sums(acc, out_ref, ids_ref[1] if rolled else None)


def last_kernel(ids_ref, got_ref, e_ref, peak_ref, out_ref, pot_ref, factor_ref, *, scale, rolled, log_count):
    rows_all = e_ref.shape[0]
    tiles = e_ref.shape[1] // LANES
    group = group_of(rows_all)
    w = spread(get_factors(got_ref, scale, ids_ref[2] if rolled else None))

    def body(i, acc):
        sums = [tree(jnp.add, [x * f for x, f in zip(load(e_ref, group_rows(i, g, group)), w)]) for g in range(group)]
        sums = [1.0 / jnp.sum(x, axis=1, keepdims=True) for x in sums]
        for g in range(group):
            rows = group_rows(i, g, group)
            factor_ref[rows, :] = jnp.broadcast_to(sums[g], (SUB, LANES))
            acc = [a + x * sums[g] for a, x in zip(acc, load(e_ref, rows))]
        return tuple(acc)

    acc = tuple(jnp.zeros((SUB, LANES), jnp.float32) for _ in range(tiles))
    acc = lax.fori_loop(0, rows_all // (group * SUB), body, acc)
    put_sums(acc, out_ref, ids_ref[1] if rolled else None)
    shape = (LANES, LANES)
    eye = lax.broadcasted_iota(jnp.int32, shape, 0) == lax.broadcasted_iota(jnp.int32, shape, 1)
    for i in range(rows_all // LANES):
        rows = slice(i * LANES, (i + 1) * LANES)
        peak, factor = (
            jnp.sum(jnp.where(eye, ref[rows, :], 0.0), axis=0, keepdims=True) for ref in (peak_ref, factor_ref)
        )
        pot_ref[i : i + 1, :] = -eps_blur * (log_count + math.log(2) * peak - jnp.log(factor))


def out_kernel(ids_ref, got_ref, e_ref, factor_ref, perm_ref, pot_ref, member_ref, *, scale, rolled):
    tiles = e_ref.shape[1] // LANES
    factors = get_factors(got_ref, scale, ids_ref[2] if rolled else None)
    w = jnp.concatenate([factors[i : i + 1, :] for i in range(tiles)], axis=1)
    v = eps_blur * jnp.log(w)
    high = v.astype(jnp.bfloat16).astype(jnp.float32)
    mid = (v - high).astype(jnp.bfloat16).astype(jnp.float32)
    low = v - high - mid
    at = lax.broadcasted_iota(jnp.int32, (16, w.shape[1]), 0)
    parts = jnp.where(at == 0, high, jnp.where(at == 1, mid, jnp.where(at == 2, low, 0.0)))
    moved = lax.dot_general(
        parts.astype(jnp.bfloat16), perm_ref[...], NT, preferred_element_type=jnp.float32
    )
    pot_ref[...] = moved[0:1, :] + moved[1:2, :] + moved[2:3, :]
    step = min(256, e_ref.shape[0])
    for i in range(0, e_ref.shape[0], step):
        tile = load(e_ref, slice(i, i + step))
        plan = jnp.concatenate([x * factor_ref[i : i + step, :] for x in tile], axis=1) * w
        member_ref[:, i : i + step] = lax.dot_general(
            perm_ref[...], plan.astype(jnp.bfloat16), NT, preferred_element_type=jnp.float32
        ).astype(member_ref.dtype)


def on_device(scenarios, rep_index):
    scen_rows, width = scenarios.shape
    n = lax.axis_size("scen")
    n_rep = lax.axis_size("rep")
    count_r = rep_index.shape[0]
    count_s = scen_rows * n
    per = count_r // n
    features = width * n_rep
    rows_out = count_r // n_rep
    rolled = per == LANES
    as_int = lambda x: x.astype(jnp.int32)

    def tied(xs, *after):
        return list(lax.optimization_barrier((tuple(xs), after))[0])

    ring = list(range(0, n, 2)) + list(range(n - 1, 0, -2))
    up = [(ring[i], ring[(i + 1) % n]) for i in range(n)]
    down = [(b, a) for a, b in up]
    at_ring = [ring.index(i) for i in range(n)]

    d = lax.axis_index("scen")
    rep = lax.axis_index("rep")
    place = jnp.where((d & 1) == 0, d >> 1, n - 1 - (d >> 1))
    back = jnp.where(place == 0, 0, n - place)
    scalars = tuple(x.astype(jnp.int32) for x in (rep & 1, place, back, rep * rows_out))
    rep_index, core, place, back, out_from = tied([rep_index, *scalars])

    scenarios, *halves = pick(rep_index, scenarios, per)
    ids = jnp.stack([core, place, back])
    wanted = lax.dynamic_slice(rep_index, (out_from,), (rows_out,), allow_negative_indices=False)

    rank = jnp.sum(as_int(rep_index[None, :] < wanted[:, None]), axis=1)
    block = rank // per
    at = sum(jnp.where(block == i, at_ring[i], 0) for i in range(n)) - place
    at = jnp.where(at < 0, at + n, at) * per + rank % per
    perm = (at[:, None] == jnp.arange(count_r, dtype=jnp.int32)[None, :]).astype(jnp.bfloat16)

    def swap(x, bit):
        return lax.ppermute(x, "rep", [(i, i ^ bit) for i in range(n_rep)])

    def rest(part, *after):
        bit = 2
        while bit < n_rep:
            got = swap(part, bit)
            if after:
                (got,) = tied([got], *after)
            part = part + got
            bit *= 2
        return part

    stages = []
    where = [None] * n

    def finish(part, *after):
        whole = rest(part, *after)
        other = swap(whole, 1)
        stages.append((whole, other))
        return whole, other

    f32 = lambda *shape: pltpu.VMEM(shape, jnp.float32)
    tiles = count_r // LANES
    to_power = -1.0 / (features * eps_blur * math.log(2))

    def start_early(pieces, stages):
        given = [s[0] for s in stages] + [s[1] for s in stages]
        return pl.pallas_call(
            functools.partial(early_kernel, pieces=pieces, scale=to_power),
            out_shape=(f32(scen_rows, len(pieces) * LANES), f32(scen_rows, LANES), f32(scen_rows, LANES)),
            in_specs=[SMEM] + [VMEM] * len(given),
            out_specs=(VMEM,) * 3,
            cost_estimate=COST,
            compiler_params=ROOM,
            name="early",
        )(ids, *kept(*given))

    ties = {}

    def tie(h, after, *xs):
        if after:
            ties.setdefault(h + after, []).extend(xs)

    sq_scen = norms(scenarios)
    shares = cost_share(ids, scenarios, sq_scen, halves)
    tie(0, 1, perm)
    a, b = halves, halves[::-1]
    a[1], b[1] = tied([a[1], b[1]], sq_scen)
    waiting = []
    for h in range(n):
        i, k = (h + 1) % 2, (h + 1) // 2
        if h:
            a[i], b[i] = (lax.ppermute(x, "scen", way) for x, way in ((a[i], up), (b[i], down)))
            a[i], b[i] = tied([a[i], b[i]], *ties.pop(h, []))
            chunks = [b[i], a[i]] if i else [a[i], b[i]]
        if h == n - 1:
            sent = cost_share(ids, scenarios, sq_scen, chunks, parts=(True,))
            shares = [*sent, *cost_share(ids, scenarios, sq_scen, chunks, parts=(False,))]
        elif h:
            sent = shares = cost_share(ids, scenarios, sq_scen, chunks)
        for g, part in waiting:
            whole, other = finish(part, *sent, *(begun if g == n - 2 else ()))
            tie(g, AFTER[n - g][1], whole)
            tie(g, AFTER[n - g][2], other)
        waiting = []
        part = shares[1] + swap(shares[0], 1)
        after = AFTER.get(n - h, AFTER[0])
        tie(h, 1, *shares)
        tie(h, after[0], part)
        if h in (n - 3, n - 2):
            waiting.append((h, part))
        else:
            whole, other = finish(part)
            tie(h, after[1], whole)
            tie(h, after[2], other)
        if h in (0, n - 1):
            where[k] = [(h, 0)]
        elif i == 1:
            where[n - k], where[k] = [(h - 1, 0), (h, 0)], [(h, 0), (h - 1, 0)]
        if h == n - 4:
            begun = start_early([w for w in where if w], stages) if rolled else ()

    own, other = [s[0] for s in stages], [s[1] for s in stages]
    if rolled:
        cut = len(stages) - 3
        order = sorted(range(n), key=lambda q: where[q][0][0] >= cut)
        pieces = [[(s - cut, at) for s, at in where[q]] for q in order if where[q][0][0] >= cut]
        late = own[cut:] + other[cut:]
    else:

        def join(xs):
            cols = []
            for piece in where:
                part = [xs[s][:, at : at + per] for s, at in piece]
                cols += part if len(part) == 1 else [part[0][:, : per // 2], part[1][:, per // 2 :]]
            return jnp.concatenate(cols, axis=1)

        order = list(range(tiles))
        pieces = [[(0, i * LANES)] for i in order]
        late = [join(own), join(other)]
        begun = start_early(pieces[: tiles // 2], [late])
        pieces = pieces[tiles // 2 :]

    sums = f32(n, tiles, LANES)

    def exchange(x):
        if not rolled:
            x = jnp.roll(x.reshape(n, count_r), place * per, axis=1).reshape(x.shape)
        x = lax.all_to_all(x, "scen", 0, 0, tiled=False)
        if not rolled:
            x = jnp.roll(x.reshape(n, count_r), -place * per, axis=1).reshape(x.shape)
        return x

    e, peak, x = pl.pallas_call(
        functools.partial(late_kernel, pieces=pieces, order=order, scale=to_power, rolled=rolled),
        out_shape=(f32(scen_rows, count_r), f32(scen_rows, LANES), sums),
        in_specs=[SMEM] + [VMEM] * (3 + len(late)),
        out_specs=(VMEM,) * 3,
        compiler_params=ROOM,
        name="late",
    )(ids, *kept(*begun, *late))
    scale = count_s / count_r
    for _ in range(ITERS - 2):
        x = pl.pallas_call(
            functools.partial(step_kernel, scale=scale, rolled=rolled),
            out_shape=sums,
            in_specs=[SMEM, VMEM, VMEM],
            out_specs=VMEM,
            compiler_params=ROOM,
            name="step",
        )(ids, *kept(exchange(x), e))
    x, scen_pot, factor = pl.pallas_call(
        functools.partial(last_kernel, scale=scale, rolled=rolled, log_count=math.log(count_s)),
        out_shape=(
            sums,
            jax.ShapeDtypeStruct((scen_rows // LANES, LANES), jnp.float32),
            f32(scen_rows, LANES),
        ),
        in_specs=[SMEM] + [VMEM] * 3,
        out_specs=(VMEM,) * 3,
        compiler_params=ROOM,
        name="last",
    )(ids, *kept(exchange(x), e, peak))
    rep_pot, member = pl.pallas_call(
        functools.partial(out_kernel, scale=scale, rolled=rolled),
        out_shape=(
            jax.ShapeDtypeStruct((1, rows_out), jnp.float32),
            jax.ShapeDtypeStruct((rows_out, scen_rows), jnp.bfloat16),
        ),
        in_specs=[SMEM] + [VMEM] * 4,
        out_specs=(VMEM, VMEM),
        compiler_params=ROOM,
        name="out",
    )(ids, *kept(exchange(x), e, factor, perm))
    return scen_pot.reshape(scen_rows), rep_pot.reshape(rows_out), member


def solution(mesh):
    return jax.shard_map(
        on_device,
        mesh=mesh,
        in_specs=(P("scen", "rep"), P()),
        out_specs=(P("scen"), P("rep"), P("rep", "scen")),
        check_vma=False,
    )
```
